256 devices in a mesh: dp: 32 (over x, y, z_hi), tensor: 8 (over z_lo, core).
Axes of the slice: x: 4, y: 4, z: 8 (z_hi: 2, z_lo: 4; z = z_hi * 4 + z_lo), core: 2. Of those that a mesh axis runs over, the one named last changes fastest.
Arguments:
- hidden: bfloat16 [32768, 8192], P(('dp', 'tensor')), may hold values from -24 to 24
- w_key: bfloat16 [8192, 1024], P(None, 'tensor'), may hold values from -0.0625 to 0.0625
- value_weight: bfloat16 [8192, 1024], P(None, 'tensor'), may hold values from -0.0625 to 0.0625
- value_down_factor: bfloat16 [32, 8192], replicated, may hold values from -0.0625 to 0.0625
- value_up_factor: bfloat16 [32, 1024], P(None, 'tensor'), may hold values from -0.5 to 0.5
- mag_value: float32 [1024], P('tensor'), may hold values from 0.5 to 2
- queries: bfloat16 [32768, 4096], P('dp', 'tensor'), may hold values from -1200 to 1200
- grad_attn: bfloat16 [32768, 4096], P('dp', 'tensor'), may hold values from -6 to 6
Outputs:
- grad_hidden: bfloat16 [32768, 8192], P(('dp', 'tensor'))
- grad_down: float32 [32, 8192], P(None, ('dp', 'tensor'))
- grad_up: float32 [32, 1024], P(None, 'tensor')
- grad_mag: float32 [1024], P('tensor')
The draws below stay inside these ranges and needn't reach their ends.
All inputs are finite; a program needn't handle non-finite values.
Results may differ from the reference program's by a relative error of at most 0.04.
Values may be sent and summed in bfloat16 or wider, within the bound.
No kernel may reach another device: no remote copies, remote signals or barrier semaphores. Data moves between devices by JAX's collectives and lax.ppermute only.
A program may use at most 192 MiB of HBM per device.

```python
import math
import jax
import jax.numpy as jnp
from jax import lax

D = 8192
HD = 128
KVH = 8
QH = 32
R = 32
SEQ = 1024
TOKENS = 32768
KV = 1024
QW = 4096
N_DP = 32
N_TENSOR = 8


def draw_queries(key, part):
    key = jax.random.fold_in(key, 7)
    entry_key, pick_key, level_key, spot_key = jax.random.split(key, 4)
    entries = jnp.clip(jax.random.normal(entry_key, (TOKENS, QH, HD), jnp.float32), -6.0, 6.0)
    strength = jnp.exp(jax.random.uniform(level_key, (TOKENS, QH, 1), jnp.float32, math.log(8.0), math.log(100.0)))
    forced_level = 160.0
    chosen = jax.random.bernoulli(pick_key, 0.125, (TOKENS, QH, 1))
    seq_count = TOKENS // SEQ
    forced_spot = jax.random.randint(spot_key, (seq_count, 1, QH), SEQ // 2, SEQ)
    position = jnp.arange(SEQ)[None, :, None]
    forced = (position == forced_spot).reshape(TOKENS, QH, 1)
    row_scale = jnp.where(forced, forced_level, jnp.where(chosen, strength, 1.0))
    return (entries * row_scale).reshape(TOKENS, QH * HD).astype(jnp.bfloat16)


def with_spikes(values, own_key, source, target, shards_of, factor):
    owner, partner = [(jnp.arange(values.shape[dim]) // (values.shape[dim] // shards_of)).reshape([-1 if axis == dim else 1 for axis in range(values.ndim)]) for dim in (source, target)]
    chosen = jax.random.permutation(own_key, shards_of)[partner]
    strong = (owner == chosen) | (owner == (partner + shards_of // 2) % shards_of)
    return jnp.where(strong, factor * values, values)


def levels(rng, shape, shards, smallest, high):
    factor_of = 1.0
    for dim, blocks in shards:
        steps = jax.random.uniform(jax.random.fold_in(jax.random.fold_in(rng, 6), dim), (blocks,), jnp.float32, smallest / len(shards), high / len(shards))
        factor_of = factor_of * jnp.repeat(jnp.exp(steps), shape[dim] // blocks).reshape((-1,) + (1,) * (len(shape) - 1 - dim))
    return factor_of


def bell_draw(stream_key, shape, width, most, pieces=(), kind=jnp.bfloat16):
    values = width * jax.random.normal(stream_key, shape, jnp.float32)
    if pieces:
        values = values * levels(stream_key, shape, pieces, -0.22, 0.18)
    return jnp.clip(values, -most, most).astype(kind)


def bell_draw_with(own_key, shape, width, reach, pieces, heavy, kind=jnp.bfloat16):
    drawn = width * jax.random.normal(own_key, shape, jnp.float32)
    if pieces:
        drawn = drawn * levels(own_key, shape, pieces, -0.22, 0.18)
    return jnp.clip(with_spikes(drawn, jax.random.fold_in(own_key, 3), *heavy), -reach, reach).astype(kind)


def setup_inputs(seed: int = 0) -> dict:
    arg_keys = jax.random.split(jax.random.key(seed), 9)
    hidden = bell_draw_with(arg_keys[0], (TOKENS, D), 1.0, 24.0, ((0, 256),), (0, 1, 256, 6.0))
    w_key = bell_draw(arg_keys[1], (D, KV), D ** -0.5, 0.0625, ((1, 8),))
    value_weight = bell_draw(arg_keys[2], (D, KV), D ** -0.5, 0.0625, ((1, 8),))
    value_down_factor = bell_draw(arg_keys[3], (R, D), D ** -0.5, 0.0625)
    value_up_factor = bell_draw(arg_keys[4], (R, KV), (4 * R) ** -0.5, 0.5, ((1, 8),))
    mag_value = jnp.clip(jnp.exp(math.log(2.0) - 1.3862944 * jax.random.uniform(arg_keys[5], (KV,), jnp.float32) ** levels(arg_keys[5], (KV,), ((0, 8),), -0.2, 0.2)), 0.5, 2.0)
    queries = draw_queries(jax.random.fold_in(arg_keys[8], 71), 0)
    grad_attn = bell_draw(arg_keys[7], (TOKENS, QW), 1.0, 6.0, ((0, 32), (1, 8)))
    return dict(hidden=hidden, w_key=w_key, value_weight=value_weight, value_down_factor=value_down_factor, value_up_factor=value_up_factor, mag_value=mag_value, queries=queries, grad_attn=grad_attn)


adapter_scale = 2.0
rope_base = 500000.0

def rounded_output(values):
    return lax.optimization_barrier(values.astype(jnp.bfloat16))

def rope_tables(length, head_size):
    half_size = head_size // 2
    frequency = rope_base ** (-(jnp.arange(half_size, dtype=jnp.float32) * 2.0 / head_size))
    angles = jnp.arange(length, dtype=jnp.float32)[:, None] * frequency[None, :]
    return (jnp.cos(angles), jnp.sin(angles))

def rotate(vectors, cosine, sine_table, head_size):
    row_count = vectors.shape[0]
    head_count = vectors.shape[1] // head_size
    half_size = head_size // 2
    shaped = vectors.reshape(row_count, head_count, head_size)
    first_half = shaped[:, :, :half_size]
    second_half = shaped[:, :, half_size:]
    cos_part = cosine[:, None, :]
    sin_part = sine_table[:, None, :]
    joined = jnp.concatenate([first_half * cos_part - second_half * sin_part, second_half * cos_part + first_half * sin_part], axis=2)
    return joined.reshape(row_count, head_count * head_size)

def unrotate(gradients, cosine, sine_table, head_size):
    row_count = gradients.shape[0]
    head_count = gradients.shape[1] // head_size
    half_size = head_size // 2
    shaped = gradients.reshape(row_count, head_count, head_size)
    first_half = shaped[:, :, :half_size]
    second_half = shaped[:, :, half_size:]
    cos_part = cosine[:, None, :]
    sin_part = sine_table[:, None, :]
    joined = jnp.concatenate([first_half * cos_part + second_half * sin_part, second_half * cos_part - first_half * sin_part], axis=2)
    return joined.reshape(row_count, head_count * head_size)

def head_backward(query_group, grad_group, key_head, value_head, inv_sqrt):
    length = key_head.shape[0]
    query_wide = query_group.astype(jnp.float32)
    grad_wide = grad_group.astype(jnp.float32)
    key_wide = key_head.astype(jnp.float32)
    value_wide = value_head.astype(jnp.float32)
    scores = jnp.einsum('qgd,kd->gqk', query_wide, key_wide, precision=lax.Precision.HIGHEST) * inv_sqrt
    position = jnp.arange(length)
    allowed = position[None, :] <= position[:, None]
    scores = jnp.where(allowed[None], scores, -1e+30)
    attn_probs = jax.nn.softmax(scores, axis=-1)
    attn_wide = rounded_output(attn_probs).astype(jnp.float32)
    outputs = jnp.einsum('gqk,kd->gqd', attn_wide, value_wide)
    row_delta = lax.optimization_barrier(jnp.sum(jnp.transpose(grad_wide, (1, 0, 2)) * outputs, axis=-1))
    probs_grad = jnp.einsum('qgd,kd->gqk', grad_wide, value_wide)
    scores_grad = rounded_output(attn_probs * (probs_grad - row_delta[:, :, None]) * inv_sqrt).astype(jnp.float32)
    key_grad = jnp.einsum('gqk,qgd->kd', scores_grad, query_wide)
    value_grad = jnp.einsum('gqk,qgd->kd', attn_wide, grad_wide)
    return (key_grad, value_grad)

def reference(hidden, w_key, value_weight, value_down_factor, value_up_factor, mag_value, queries, grad_attn):
    low_rank_update = jnp.dot(value_down_factor.T, value_up_factor, preferred_element_type=jnp.float32)
    merged_weight = value_weight.astype(jnp.float32) + adapter_scale * low_rank_update
    col_norms = jnp.sqrt(lax.optimization_barrier(jnp.sum(merged_weight * merged_weight, axis=0)))
    col_scale = mag_value / col_norms
    cosine, sine_table = rope_tables(SEQ, HD)
    group_size = QH // KVH
    group_width = KV // N_TENSOR
    inv_sqrt = HD ** (-0.5)

    def one_sequence(sequence):
        block_of_tokens, query_seq, grad_seq = sequence
        down_product = rounded_output(jnp.dot(block_of_tokens, value_down_factor.T, preferred_element_type=jnp.float32))
        key_proj = jnp.dot(block_of_tokens, w_key, preferred_element_type=jnp.float32)
        base_value = rounded_output(jnp.dot(block_of_tokens, value_weight, preferred_element_type=jnp.float32) + adapter_scale * jnp.dot(down_product, value_up_factor, preferred_element_type=jnp.float32))
        key_rot = rotate(key_proj, cosine, sine_table, HD)
        value_heads = rounded_output(col_scale * base_value.astype(jnp.float32))
        key_list = []
        value_list = []
        for head_index in range(KVH):
            head_cols = slice(head_index * HD, (head_index + 1) * HD)
            query_cols = slice(head_index * group_size * HD, (head_index + 1) * group_size * HD)
            key_grad, value_grad = head_backward(query_seq[:, query_cols].reshape(SEQ, group_size, HD), grad_seq[:, query_cols].reshape(SEQ, group_size, HD), key_rot[:, head_cols], value_heads[:, head_cols], inv_sqrt)
            key_list.append(key_grad)
            value_list.append(value_grad)
        key_rot_grad = jnp.concatenate(key_list, axis=1)
        value_grad = jnp.concatenate(value_list, axis=1)
        grad_key = rounded_output(unrotate(key_rot_grad, cosine, sine_table, HD))
        value_gradient = rounded_output(value_grad * col_scale)
        mag_term = lax.optimization_barrier(jnp.sum(value_grad * base_value.astype(jnp.float32), axis=0)) / col_norms
        right_piece = adapter_scale * jnp.dot(down_product.T, value_gradient, preferred_element_type=jnp.float32)
        rank_gradient = rounded_output(jnp.dot(value_gradient, value_up_factor.T, preferred_element_type=jnp.float32))
        summed_heads = jnp.zeros((SEQ, D), jnp.float32)
        for part_index in range(N_TENSOR):
            part_cols = slice(part_index * group_width, (part_index + 1) * group_width)
            piece_term = jnp.dot(grad_key[:, part_cols], w_key[:, part_cols].T, preferred_element_type=jnp.float32) + jnp.dot(value_gradient[:, part_cols], value_weight[:, part_cols].T, preferred_element_type=jnp.float32)
            summed_heads = summed_heads + rounded_output(piece_term).astype(jnp.float32)
        token_gradient = (summed_heads + adapter_scale * jnp.dot(rank_gradient, value_down_factor, preferred_element_type=jnp.float32)).astype(jnp.bfloat16)
        down_piece = adapter_scale * jnp.dot(rank_gradient.T, block_of_tokens, preferred_element_type=jnp.float32)
        return (token_gradient, down_piece, right_piece, mag_term)
    results = lax.map(one_sequence, (hidden.reshape(N_DP, SEQ, D), queries.reshape(N_DP, SEQ, QW), grad_attn.reshape(N_DP, SEQ, QW)))
    grad_hidden = results[0].reshape(TOKENS, D)
    grad_down = lax.optimization_barrier(jnp.sum(results[1], axis=0))
    grad_up = lax.optimization_barrier(jnp.sum(results[2], axis=0))
    grad_mag = lax.optimization_barrier(jnp.sum(results[3], axis=0))
    return (grad_hidden, grad_down, grad_up, grad_mag)
```

```python
import jax
import jax.numpy as jnp
import numpy as np
from jax import lax
from jax.experimental import pallas as pl
from jax.experimental.pallas import tpu as pltpu
from jax.sharding import Mesh, PartitionSpec as P

HD = 128
D = 8192
SEQ = 1024
RANK = 32
PAIR = 256
KB = 512
QB = 256
GROUP = 4
SCALE = 2.0
ROPE_BASE = 500000.0
LOG2E = 1.4426950408889634
INV_SQRT = HD ** (-0.5)
MIB = 1024 * 1024
BF = jnp.bfloat16
F32 = jnp.float32
NT = (((1,), (1,)), ((), ()))
TN = (((0,), (0,)), ((), ()))
EVERY = ("x", "y", "zh", "zl", "core")
DP = ("x", "y", "zh")


def rope_tables():
    half = HD // 2
    frequency = ROPE_BASE ** (-(jnp.arange(half, dtype=F32) * 2.0 / HD))
    angles = jnp.arange(SEQ, dtype=F32)[:, None] * frequency[None, :]
    cosine, sine = jnp.cos(angles), jnp.sin(angles)
    return jnp.concatenate([cosine, cosine], 1), jnp.concatenate([-sine, sine], 1)


def smem():
    return pl.BlockSpec(memory_space=pltpu.SMEM)


def whole(shape):
    return pl.BlockSpec(shape, lambda *_: (0,) * len(shape))


def params(limit):
    return pltpu.CompilerParams(vmem_limit_bytes=limit * MIB)


def cost(flops, moved, trans=0):
    return pl.CostEstimate(flops=flops, bytes_accessed=moved, transcendentals=trans)


def project_kernel(place, hid, own_key, own_val, far, down, ups, cos, sin, out, acc):
    step = pl.program_id(0)

    @pl.when(step == 0)
    def _():
        acc[...] = jnp.zeros_like(acc)

    rows = hid[...]
    own = jnp.concatenate([own_key[...], own_val[...]], axis=1)
    acc[0] += jnp.dot(rows, own, preferred_element_type=F32)
    for r in range(1, 4):
        acc[r] += jnp.dot(rows, far[:, (r - 1) * 256 : r * 256], preferred_element_type=F32)

    @pl.when(step == pl.num_programs(0) - 1)
    def _():
        for r in range(4):
            key = acc[r, :, :HD]
            turned = key * cos[...] + pltpu.roll(key, HD // 2, 1) * sin[...]
            turned = turned * (INV_SQRT * LOG2E)
            high = turned.astype(BF)
            low = (turned - high.astype(F32)).astype(BF)
            lifted = jnp.dot(down[...], ups[r], preferred_element_type=F32)
            base = (acc[r, :, HD:] + SCALE * lifted).astype(BF)
            slot = lax.rem(place[0] + r, 4)
            out[slot] = jnp.concatenate([high, low, base], axis=1)


def project(place, pair, w_key, w_val, far, down, ups, cos, sin):
    return pl.pallas_call(
        project_kernel,
        grid=(D // KB,),
        in_specs=[
            smem(),
            pl.BlockSpec((PAIR, KB), lambda k: (0, k)),
            pl.BlockSpec((KB, HD), lambda k: (k, 0)),
            pl.BlockSpec((KB, HD), lambda k: (k, 0)),
            pl.BlockSpec((KB, 6 * HD), lambda k: (k, 0)),
            whole((PAIR, RANK)),
            whole((4, RANK, HD)),
            whole((PAIR, HD)),
            whole((PAIR, HD)),
        ],
        out_specs=whole((4, PAIR, 3 * HD)),
        out_shape=jax.ShapeDtypeStruct((4, PAIR, 3 * HD), BF),
        scratch_shapes=[pltpu.VMEM((4, PAIR, 2 * HD), F32)],
        compiler_params=params(32),
        cost_estimate=cost(2 * PAIR * D * 1024, 20 * MIB),
        name="project",
    )(place, pair, w_key, w_val, far, down, ups, cos, sin)


def attend_kernel(query, grad, rows, col_scale, down, cos, sin, grads, up_grad, mag_grad, vals, dkey, dval):
    head = pl.program_id(0)

    @pl.when(head == 0)
    def _():
        vals[...] = (rows[:, 2 * HD :].astype(F32) * col_scale[...]).astype(BF)
        dkey[...] = jnp.zeros_like(dkey)
        dval[...] = jnp.zeros_like(dval)

    for block in range(SEQ // QB):
        stop = (block + 1) * QB
        here = slice(block * QB, stop)
        q = query[here, :]
        g = grad[here, :]
        qq = jnp.concatenate([q, q], axis=1)
        scores = lax.dot_general(rows[:stop, : 2 * HD], qq, NT, preferred_element_type=F32)
        key_at = lax.broadcasted_iota(jnp.int32, (QB, QB), 0)
        query_at = lax.broadcasted_iota(jnp.int32, (QB, QB), 1)
        edge = jnp.where(key_at <= query_at, scores[block * QB :], -1e30)
        if block:
            scores = jnp.concatenate([scores[: block * QB], edge], axis=0)
        else:
            scores = edge
        powers = jnp.exp2(scores - jnp.max(scores, axis=0, keepdims=True))
        attn = powers * (1.0 / jnp.sum(powers, axis=0, keepdims=True))
        half = attn.astype(BF)
        pgrad = lax.dot_general(vals[:stop], g, NT, preferred_element_type=F32)
        delta = jnp.sum(half.astype(F32) * pgrad, axis=0, keepdims=True)
        sgrad = (attn * (pgrad - delta)).astype(BF)
        dval[:stop] += jnp.dot(half, g, preferred_element_type=F32)
        dkey[:stop] += jnp.dot(sgrad, q, preferred_element_type=F32)

    @pl.when(head == pl.num_programs(0) - 1)
    def _():
        dk = dkey[...] * INV_SQRT
        dk = dk * cos[...] - pltpu.roll(dk, HD // 2, 1) * sin[...]
        dv = dval[...]
        gv = (dv * col_scale[...]).astype(BF)
        grads[:, :HD] = dk.astype(BF)
        grads[:, HD:] = gv
        up_grad[...] = SCALE * lax.dot_general(down[...], gv, TN, preferred_element_type=F32)
        total = jnp.sum(dv * rows[:, 2 * HD :].astype(F32), axis=0, keepdims=True)
        mag_grad[...] = jnp.broadcast_to(total, mag_grad.shape)


def attend(queries, grad_attn, rows, col_scale, down, cos, sin):
    return pl.pallas_call(
        attend_kernel,
        grid=(GROUP,),
        in_specs=[
            pl.BlockSpec((SEQ, HD), lambda h: (0, h)),
            pl.BlockSpec((SEQ, HD), lambda h: (0, h)),
            whole((SEQ, 3 * HD)),
            whole((1, HD)),
            whole((SEQ, RANK)),
            whole((SEQ, HD)),
            whole((SEQ, HD)),
        ],
        out_specs=[whole((SEQ, 2 * HD)), whole((RANK, HD)), whole((8, HD))],
        out_shape=[
            jax.ShapeDtypeStruct((SEQ, 2 * HD), BF),
            jax.ShapeDtypeStruct((RANK, HD), F32),
            jax.ShapeDtypeStruct((8, HD), F32),
        ],
        scratch_shapes=[
            pltpu.VMEM((SEQ, HD), BF),
            pltpu.VMEM((SEQ, HD), F32),
            pltpu.VMEM((SEQ, HD), F32),
        ],
        compiler_params=params(40),
        cost_estimate=cost(5 * 2 * GROUP * SEQ * SEQ * HD, 6 * MIB, GROUP * SEQ * SEQ),
        name="attend",
    )(queries, grad_attn, rows, col_scale, down, cos, sin)


def rank_kernel(place, grads, ups, out):
    total = jnp.zeros((PAIR, RANK), F32)
    for r in range(4):
        slot = lax.rem(place[0] + r, 4)
        total += lax.dot_general(grads[slot, :, HD:], ups[r], NT, preferred_element_type=F32)
    out[...] = total


def rank_part(place, grads, ups):
    return pl.pallas_call(
        rank_kernel,
        in_specs=[smem(), whole((4, PAIR, 2 * HD)), whole((4, RANK, HD))],
        out_specs=whole((PAIR, RANK)),
        out_shape=jax.ShapeDtypeStruct((PAIR, RANK), F32),
        compiler_params=params(16),
        cost_estimate=cost(2 * PAIR * 512 * RANK, MIB),
        name="rank_part",
    )(place, grads, ups)


def back_kernel(place, grads, own_key, own_val, far, mine, theirs, left):
    step = pl.program_id(0)

    @pl.when(step == 0)
    def _():
        first = pl.multiple_of(place[1] * 128, 128)
        second = pl.multiple_of(128 - place[1] * 128, 128)
        for r in range(4):
            slot = lax.rem(place[0] + r, 4)
            left[:128, r * 256 : (r + 1) * 256] = grads[slot, pl.ds(first, 128), :]
            left[128:, r * 256 : (r + 1) * 256] = grads[slot, pl.ds(second, 128), :]

    weights = jnp.concatenate([own_key[...], own_val[...], far[...]], axis=1)
    part = lax.dot_general(left[...], weights, NT, preferred_element_type=F32)
    mine[...] = part[:128]
    theirs[...] = part[128:].astype(BF)


def back(place, grads, w_key, w_val, far):
    return pl.pallas_call(
        back_kernel,
        grid=(D // KB,),
        in_specs=[
            smem(),
            whole((4, PAIR, 2 * HD)),
            pl.BlockSpec((KB, HD), lambda k: (k, 0)),
            pl.BlockSpec((KB, HD), lambda k: (k, 0)),
            pl.BlockSpec((KB, 6 * HD), lambda k: (k, 0)),
        ],
        out_specs=[
            pl.BlockSpec((128, KB), lambda k: (0, k)),
            pl.BlockSpec((128, KB), lambda k: (0, k)),
        ],
        out_shape=[jax.ShapeDtypeStruct((128, D), F32), jax.ShapeDtypeStruct((128, D), BF)],
        scratch_shapes=[pltpu.VMEM((PAIR, 1024), BF)],
        compiler_params=params(32),
        cost_estimate=cost(2 * PAIR * D * 1024, 23 * MIB),
        name="back",
    )(place, grads, w_key, w_val, far)


def down_kernel(place, rank, hid, out):
    part = SCALE * lax.dot_general(rank[...], hid[...], TN, preferred_element_type=F32)
    lane = lax.broadcasted_iota(jnp.int32, (8, HD), 1) // 32
    core = place[1]
    for tile in range(part.shape[1] // HD):
        regs = [part[8 * i : 8 * i + 8, tile * HD : (tile + 1) * HD] for i in range(4)]
        for pick in range(2):
            column = 2 * pick + core
            block = jnp.zeros((8, HD), F32)
            for i in range(4):
                moved = pltpu.roll(regs[i], lax.rem((i - column + 4) * 32, HD), 1)
                block = jnp.where(lane == i, moved, block)
            out[2 * tile + pick] = block


def down_part(place, rank, pair):
    wide = 1024
    return pl.pallas_call(
        down_kernel,
        grid=(D // wide,),
        in_specs=[smem(), whole((PAIR, RANK)), pl.BlockSpec((PAIR, wide), lambda k: (0, k))],
        out_specs=pl.BlockSpec((wide // 64, 8, HD), lambda k: (k, 0, 0)),
        out_shape=jax.ShapeDtypeStruct((128, 8, HD), F32),
        compiler_params=params(16),
        cost_estimate=cost(2 * PAIR * D * RANK, 5 * MIB),
        name="down_part",
    )(place, rank, pair)


def join_kernel(place, rank, mine, theirs, factor, out):
    own = rank[pl.ds(pl.multiple_of(place[1] * 128, 128), 128), :]
    adapter = SCALE * jnp.dot(own, factor[...], preferred_element_type=F32)
    out[...] = (mine[...] + theirs[...].astype(F32) + adapter).astype(BF)


def join(place, rank, mine, theirs, factor):
    wide = 2048
    return pl.pallas_call(
        join_kernel,
        grid=(D // wide,),
        in_specs=[
            smem(),
            whole((PAIR, RANK)),
            pl.BlockSpec((128, wide), lambda k: (0, k)),
            pl.BlockSpec((128, wide), lambda k: (0, k)),
            pl.BlockSpec((RANK, wide), lambda k: (0, k)),
        ],
        out_specs=pl.BlockSpec((128, wide), lambda k: (0, k)),
        out_shape=jax.ShapeDtypeStruct((128, D), BF),
        compiler_params=params(16),
        cost_estimate=cost(2 * 128 * RANK * D, 9 * MIB),
        name="join",
    )(place, rank, mine, theirs, factor)


def gather_weights(w_key, w_val, up):
    at = (lax.axis_index("x") * 4 + lax.axis_index("y")) * 512
    seed = jnp.concatenate(
        [lax.dynamic_slice(w_key, (at, 0), (512, HD)), lax.dynamic_slice(w_val, (at, 0), (512, HD))], axis=1
    )
    seed = jnp.concatenate([seed, jnp.pad(up, ((0, 0), (0, HD)))], axis=0)
    got = []
    for shift in (-1, -2, 1):
        got.append(lax.ppermute(seed, ("zh", "zl"), [(i, (i + shift) % 8) for i in range(8)]))
    far = lax.all_gather(jnp.concatenate([g[:512] for g in got], axis=1), ("x", "y"), axis=0, tiled=True)
    ups = jnp.stack([up] + [g[512:, :HD] for g in got])
    return far, ups


def shards(hidden, w_key, w_val, factor, up, mag, queries, grad_attn):
    zl, core = lax.axis_index("zl"), lax.axis_index("core")
    place = jnp.stack([zl, core]).astype(jnp.int32)
    swap = [(0, 1), (1, 0)]
    far, ups = gather_weights(w_key, w_val, up)
    other = lax.ppermute(hidden, "core", swap)
    pair = jnp.where(
        core == 0, jnp.concatenate([hidden, other], axis=0), jnp.concatenate([other, hidden], axis=0)
    )
    down = lax.dot_general(pair, factor, NT, preferred_element_type=F32).astype(BF)
    all_down = lax.all_to_all(
        jnp.broadcast_to(down[None], (4, PAIR, RANK)), "zl", 0, 0, tiled=True
    ).reshape(SEQ, RANK)
    merged = w_val.astype(F32) + SCALE * lax.dot_general(factor, up, TN, preferred_element_type=F32)
    norms = jnp.sqrt(jnp.sum(merged * merged, axis=0))
    col_scale = (mag / norms).reshape(1, HD)
    cos, sin = rope_tables()
    cos_here = lax.dynamic_slice(cos, (zl * PAIR, 0), (PAIR, HD))
    sin_here = lax.dynamic_slice(sin, (zl * PAIR, 0), (PAIR, HD))
    rows = project(place, pair, w_key, w_val, far, down, ups, cos_here, sin_here)
    rows = lax.all_to_all(rows, "zl", 0, 0, tiled=True).reshape(SEQ, 3 * HD)
    grads, up_grad, mag_grad = attend(queries, grad_attn, rows, col_scale, all_down, cos, sin)
    grads = lax.all_to_all(grads.reshape(4, PAIR, 2 * HD), "zl", 0, 0, tiled=True)
    rank = rank_part(place, grads, ups)
    rank = (rank + lax.ppermute(rank, "core", swap)).astype(BF)
    mine, theirs = back(place, grads, w_key, w_val, far)
    theirs = lax.ppermute(theirs, "core", swap)
    small = jnp.concatenate([up_grad, mag_grad / norms], axis=0)
    small = lax.all_to_all(jnp.broadcast_to(small[None], (32, 40, HD)), DP, 0, 0, tiled=True)
    small = jnp.sum(small, axis=0)
    pieces = lax.all_to_all(down_part(place, rank, pair), DP + ("zl",), 0, 0, tiled=True)
    grad_down = jnp.sum(pieces, axis=0).reshape(8, 4, 32).transpose(1, 0, 2).reshape(RANK, 32)
    grad_hidden = join(place, rank, mine, theirs, factor)
    return grad_hidden, grad_down, small[:RANK], small[RANK]


def solution(mesh):
    fine = Mesh(np.asarray(mesh.devices).reshape(4, 4, 2, 4, 2), EVERY)
    tensor = ("zl", "core")
    return jax.shard_map(
        shards,
        mesh=fine,
        in_specs=(
            P(EVERY, None),
            P(None, tensor),
            P(None, tensor),
            P(),
            P(None, tensor),
            P(tensor),
            P(DP, tensor),
            P(DP, tensor),
        ),
        out_specs=(P(EVERY, None), P(None, EVERY), P(None, tensor), P(tensor)),
        check_vma=False,
    )
```

```python
import jax
import jax.numpy as jnp
import numpy as np
from jax import lax
from jax.experimental import pallas as pl
from jax.experimental.pallas import tpu as pltpu
from jax.sharding import Mesh, PartitionSpec as P

HD = 128
D = 8192
SEQ = 1024
RANK = 32
PAIR = 256
NEAR = 4096
CROSS = 2048
LINE = 2048
CHUNK = 1024
QB = 256
GROUP = 4
SCALE = 2.0
ROPE_BASE = 500000.0
LOG2E = 1.4426950408889634
INV_SQRT = HD ** (-0.5)
MIB = 1024 * 1024
BF = jnp.bfloat16
F32 = jnp.float32
NT = (((1,), (1,)), ((), ()))
TN = (((0,), (0,)), ((), ()))
EVERY = ("x", "y", "zh", "zl", "core")
DP = ("x", "y", "zh")


def rope_tables():
    half = HD // 2
    frequency = ROPE_BASE ** (-(jnp.arange(half, dtype=F32) * 2.0 / HD))
    angles = jnp.arange(SEQ, dtype=F32)[:, None] * frequency[None, :]
    cosine, sine = jnp.cos(angles), jnp.sin(angles)
    return jnp.concatenate([cosine, cosine], 1), jnp.concatenate([-sine, sine], 1)


def smem():
    return pl.BlockSpec(memory_space=pltpu.SMEM)


def whole(shape):
    return pl.BlockSpec(shape, lambda *_: (0,) * len(shape))


def params(limit):
    return pltpu.CompilerParams(vmem_limit_bytes=limit * MIB)


def cost(flops, moved, trans=0):
    return pl.CostEstimate(flops=flops, bytes_accessed=moved, transcendentals=trans)


def any_ref():
    return pl.BlockSpec(memory_space=pl.ANY)


def start_all(copies):
    for copy in copies:
        copy.start()
    return copies


def wait_all(copies):
    for copy in copies:
        copy.wait()


def near_copies(base, own_key, own_val, far, weights, sems):
    chunks = []
    for i in range(far.shape[0] // CHUNK):
        here = pl.ds(i * CHUNK, CHUNK)
        there = pl.ds(base + i * CHUNK, CHUNK)
        chunks.append(
            [
                pltpu.make_async_copy(own_key.at[there, :], weights.at[here, pl.ds(0, HD)], sems.at[0, i]),
                pltpu.make_async_copy(own_val.at[there, :], weights.at[here, pl.ds(HD, HD)], sems.at[1, i]),
                pltpu.make_async_copy(far.at[here, :], weights.at[here, pl.ds(256, 768)], sems.at[2, i]),
            ]
        )
    return chunks


def line_copies(base, first, own_key, own_val, one, two_a, two_b, three, weights, sems):
    chunks = []
    size = LINE // 2
    for i, two in enumerate((two_a.at[pl.ds(RANK, size), :], two_b)):
        here = pl.ds(first + i * size, size)
        there = pl.ds(base + i * size, size)
        near = pl.ds(RANK + i * size, size)
        chunks.append(
            [
                pltpu.make_async_copy(own_key.at[there, :], weights.at[here, pl.ds(0, HD)], sems.at[0, i]),
                pltpu.make_async_copy(own_val.at[there, :], weights.at[here, pl.ds(HD, HD)], sems.at[1, i]),
                pltpu.make_async_copy(one.at[near, :], weights.at[here, pl.ds(256, 256)], sems.at[2, i]),
                pltpu.make_async_copy(two, weights.at[here, pl.ds(512, 256)], sems.at[3, i]),
                pltpu.make_async_copy(three.at[near, :], weights.at[here, pl.ds(768, 256)], sems.at[4, i]),
            ]
        )
    return chunks


def pair_copies(pair, hid, base, count, sem):
    size = hid.shape[1] // count
    return [
        pltpu.make_async_copy(
            pair.at[:, pl.ds(base + i * size, size)], hid.at[:, pl.ds(i * size, size)], sem.at[i]
        )
        for i in range(count)
    ]


def multiply(acc, chunks, hid_chunks, hid, weights):
    size = hid.shape[1] // len(chunks)
    for i, chunk in enumerate(chunks):
        wait_all(chunk + [hid_chunks[i]])
        here = slice(i * size, (i + 1) * size)
        term = jnp.dot(hid[:, here], weights[here, :], preferred_element_type=F32)
        acc = term if acc is None else acc + term
    return acc


def project_line_kernel(
    pair, own_key, own_val, cross, one, two_a, two_b, three, out, hid, weights, hid_sem, sems, line_sems
):
    chunks = near_copies(NEAR, own_key, own_val, cross, weights, sems)
    chunks += line_copies(
        NEAR + CROSS, CROSS, own_key, own_val, one, two_a, two_b, three, weights, line_sems
    )
    hid_chunks = pair_copies(pair, hid, NEAR, 4, hid_sem)
    for i in range(4):
        start_all(chunks[i] + [hid_chunks[i]])
    out[...] = multiply(None, chunks, hid_chunks, hid, weights)


def project_line(pair, w_key, w_val, cross, line):
    return pl.pallas_call(
        project_line_kernel,
        in_specs=[any_ref()] * 8,
        out_specs=whole((PAIR, 1024)),
        out_shape=jax.ShapeDtypeStruct((PAIR, 1024), F32),
        scratch_shapes=[
            pltpu.VMEM((PAIR, CROSS + LINE), BF),
            pltpu.VMEM((CROSS + LINE, 1024), BF),
            pltpu.SemaphoreType.DMA((4,)),
            pltpu.SemaphoreType.DMA((3, 2)),
            pltpu.SemaphoreType.DMA((5, 2)),
        ],
        compiler_params=params(60),
        cost_estimate=cost(2 * PAIR * (CROSS + LINE) * 1024, 11 * MIB),
        name="project_line",
    )(pair, w_key, w_val, cross, *line)


def project_kernel(
    place, pair, own_key, own_val, far, so_far, down, ups, cos, sin, out, hid, weights, hid_sem, sems
):
    count = NEAR // CHUNK
    chunks = near_copies(0, own_key, own_val, far, weights, sems)
    hid_chunks = pair_copies(pair, hid, 0, count, hid_sem)
    for i in range(count):
        start_all(chunks[i] + [hid_chunks[i]])
    acc = multiply(so_far[...], chunks, hid_chunks, hid, weights)
    for r in range(4):
        key = acc[:, r * 256 : r * 256 + HD]
        turned = key * cos[...] + pltpu.roll(key, HD // 2, 1) * sin[...]
        turned = turned * (INV_SQRT * LOG2E)
        high = turned.astype(BF)
        low = (turned - high.astype(F32)).astype(BF)
        lifted = jnp.dot(down[...], ups[r], preferred_element_type=F32)
        base = (acc[:, r * 256 + HD : (r + 1) * 256] + SCALE * lifted).astype(BF)
        slot = lax.rem(place[0] + r, 4)
        out[slot] = jnp.concatenate([high, low, base], axis=1)


def project(place, pair, w_key, w_val, far, so_far, down, ups, cos, sin):
    count = NEAR // CHUNK
    return pl.pallas_call(
        project_kernel,
        in_specs=[
            smem(),
            any_ref(),
            any_ref(),
            any_ref(),
            any_ref(),
            whole((PAIR, 1024)),
            whole((PAIR, RANK)),
            whole((4, RANK, HD)),
            whole((PAIR, HD)),
            whole((PAIR, HD)),
        ],
        out_specs=whole((4, PAIR, 3 * HD)),
        out_shape=jax.ShapeDtypeStruct((4, PAIR, 3 * HD), BF),
        scratch_shapes=[
            pltpu.VMEM((PAIR, NEAR), BF),
            pltpu.VMEM((NEAR, 1024), BF),
            pltpu.SemaphoreType.DMA((count,)),
            pltpu.SemaphoreType.DMA((3, count)),
        ],
        compiler_params=params(60),
        cost_estimate=cost(2 * PAIR * NEAR * 1024, 14 * MIB),
        name="project",
    )(place, pair, w_key, w_val, far, so_far, down, ups, cos, sin)


def attend_kernel(query, grad, rows, col_scale, down, cos, sin, grads, up_grad, mag_grad, vals, dkey, dval):
    head = pl.program_id(0)

    @pl.when(head == 0)
    def _():
        vals[...] = (rows[:, 2 * HD :].astype(F32) * col_scale[...]).astype(BF)
        dkey[...] = jnp.zeros_like(dkey)
        dval[...] = jnp.zeros_like(dval)

    for block in range(SEQ // QB):
        stop = (block + 1) * QB
        here = slice(block * QB, stop)
        q = query[here, :]
        g = grad[here, :]
        qq = jnp.concatenate([q, q], axis=1)
        scores = lax.dot_general(rows[:stop, : 2 * HD], qq, NT, preferred_element_type=F32)
        key_at = lax.broadcasted_iota(jnp.int32, (QB, QB), 0)
        query_at = lax.broadcasted_iota(jnp.int32, (QB, QB), 1)
        edge = jnp.where(key_at <= query_at, scores[block * QB :], -1e30)
        if block:
            scores = jnp.concatenate([scores[: block * QB], edge], axis=0)
        else:
            scores = edge
        powers = jnp.exp2(scores - jnp.max(scores, axis=0, keepdims=True))
        attn = powers * (1.0 / jnp.sum(powers, axis=0, keepdims=True))
        half = attn.astype(BF)
        pgrad = lax.dot_general(vals[:stop], g, NT, preferred_element_type=F32)
        delta = jnp.sum(half.astype(F32) * pgrad, axis=0, keepdims=True)
        sgrad = (attn * (pgrad - delta)).astype(BF)
        dval[:stop] += jnp.dot(half, g, preferred_element_type=F32)
        dkey[:stop] += jnp.dot(sgrad, q, preferred_element_type=F32)

    @pl.when(head == pl.num_programs(0) - 1)
    def _():
        dk = dkey[...] * INV_SQRT
        dk = dk * cos[...] - pltpu.roll(dk, HD // 2, 1) * sin[...]
        dv = dval[...]
        gv = (dv * col_scale[...]).astype(BF)
        grads[:, :HD] = dk.astype(BF)
        grads[:, HD:] = gv
        up_grad[...] = SCALE * lax.dot_general(down[...], gv, TN, preferred_element_type=F32)
        total = jnp.sum(dv * rows[:, 2 * HD :].astype(F32), axis=0, keepdims=True)
        mag_grad[...] = jnp.broadcast_to(total, mag_grad.shape)


def attend(queries, grad_attn, rows, col_scale, down, cos, sin):
    return pl.pallas_call(
        attend_kernel,
        grid=(GROUP,),
        in_specs=[
            pl.BlockSpec((SEQ, HD), lambda h: (0, h)),
            pl.BlockSpec((SEQ, HD), lambda h: (0, h)),
            whole((SEQ, 3 * HD)),
            whole((1, HD)),
            whole((SEQ, RANK)),
            whole((SEQ, HD)),
            whole((SEQ, HD)),
        ],
        out_specs=[whole((SEQ, 2 * HD)), whole((RANK, HD)), whole((8, HD))],
        out_shape=[
            jax.ShapeDtypeStruct((SEQ, 2 * HD), BF),
            jax.ShapeDtypeStruct((RANK, HD), F32),
            jax.ShapeDtypeStruct((8, HD), F32),
        ],
        scratch_shapes=[
            pltpu.VMEM((SEQ, HD), BF),
            pltpu.VMEM((SEQ, HD), F32),
            pltpu.VMEM((SEQ, HD), F32),
        ],
        compiler_params=params(60),
        cost_estimate=cost(5 * 2 * GROUP * SEQ * SEQ * HD, 6 * MIB, GROUP * SEQ * SEQ),
        name="attend",
    )(queries, grad_attn, rows, col_scale, down, cos, sin)


def rank_kernel(place, grads, ups, out):
    total = jnp.zeros((PAIR, RANK), F32)
    for r in range(4):
        slot = lax.rem(place[0] + r, 4)
        total += lax.dot_general(grads[slot, :, HD:], ups[r], NT, preferred_element_type=F32)
    out[...] = total


def rank_part(place, grads, ups):
    return pl.pallas_call(
        rank_kernel,
        in_specs=[smem(), whole((4, PAIR, 2 * HD)), whole((4, RANK, HD))],
        out_specs=whole((PAIR, RANK)),
        out_shape=jax.ShapeDtypeStruct((PAIR, RANK), F32),
        compiler_params=params(60),
        cost_estimate=cost(2 * PAIR * 512 * RANK, MIB),
        name="rank_part",
    )(place, grads, ups)


def spread(place, grads, left):
    first = pl.multiple_of(place[1] * 128, 128)
    second = pl.multiple_of(128 - place[1] * 128, 128)
    for r in range(4):
        slot = lax.rem(place[0] + r, 4)
        left[:128, r * 256 : (r + 1) * 256] = grads[slot, pl.ds(first, 128), :]
        left[128:, r * 256 : (r + 1) * 256] = grads[slot, pl.ds(second, 128), :]


def back_chunks(chunks, left, weights, mine, theirs, part, out_sem):
    size = weights.shape[0] // len(chunks)
    leaving = []
    for i, chunk in enumerate(chunks):
        wait_all(chunk)
        here = slice(i * size, (i + 1) * size)
        part[:, here] = lax.dot_general(left[...], weights[here, :], NT, preferred_element_type=F32).astype(BF)
        cols = pl.ds(i * size, size)
        leaving += start_all(
            [
                pltpu.make_async_copy(part.at[pl.ds(0, 128), cols], mine.at[:, cols], out_sem.at[0, i]),
                pltpu.make_async_copy(part.at[pl.ds(128, 128), cols], theirs.at[:, cols], out_sem.at[1, i]),
            ]
        )
    wait_all(leaving)


def back_line_kernel(
    place, grads, own_key, own_val, cross, one, two_a, two_b, three, _, mine, theirs, left, weights, part, out_sem, sems,
    line_sems,
):
    chunks = near_copies(NEAR, own_key, own_val, cross, weights, sems)
    chunks += line_copies(
        NEAR + CROSS, CROSS, own_key, own_val, one, two_a, two_b, three, weights, line_sems
    )
    for chunk in chunks:
        start_all(chunk)
    spread(place, grads, left)
    back_chunks(chunks, left, weights, mine, theirs, part, out_sem)


def back_near_kernel(place, grads, own_key, own_val, far, _, mine, theirs, left, weights, part, out_sem, sems):
    chunks = near_copies(0, own_key, own_val, far, weights, sems)
    for chunk in chunks:
        start_all(chunk)
    spread(place, grads, left)
    back_chunks(chunks, left, weights, mine, theirs, part, out_sem)


def back(kernel, kinds, name, place, grads, w_key, w_val, others, after):
    rows = D // 2
    count = rows // CHUNK
    return pl.pallas_call(
        kernel,
        in_specs=[smem(), whole((4, PAIR, 2 * HD))] + [any_ref()] * (3 + len(others)),
        out_specs=[any_ref()] * 2,
        out_shape=[jax.ShapeDtypeStruct((128, rows), BF)] * 2,
        scratch_shapes=[
            pltpu.VMEM((PAIR, 1024), BF),
            pltpu.VMEM((rows, 1024), BF),
            pltpu.VMEM((PAIR, rows), BF),
            pltpu.SemaphoreType.DMA((2, count)),
        ]
        + [pltpu.SemaphoreType.DMA(kind) for kind in kinds],
        compiler_params=params(60),
        cost_estimate=cost(MIB, MIB),
        name=name,
    )(place, grads, w_key, w_val, *others, after)


def down_kernel(place, rank, hid, out):
    part = SCALE * lax.dot_general(rank[...], hid[...], TN, preferred_element_type=F32)
    lane = lax.broadcasted_iota(jnp.int32, (8, HD), 1) // 32
    core = place[1]
    for tile in range(part.shape[1] // HD):
        regs = [part[8 * i : 8 * i + 8, tile * HD : (tile + 1) * HD] for i in range(4)]
        blocks = []
        for pick in range(2):
            column = 2 * pick + core
            block = jnp.zeros((8, HD), F32)
            for i in range(4):
                moved = pltpu.roll(regs[i], lax.rem((i - column + 4) * 32, HD), 1)
                block = jnp.where(lane == i, moved, block)
            blocks.append(block)
        out[16 * tile : 16 * tile + 16, :] = jnp.concatenate(blocks, axis=0).astype(BF)


def down_part(place, rank, pair):
    wide = 2048
    return pl.pallas_call(
        down_kernel,
        grid=(D // wide,),
        in_specs=[smem(), whole((PAIR, RANK)), pl.BlockSpec((PAIR, wide), lambda k: (0, k))],
        out_specs=pl.BlockSpec((wide // 8, HD), lambda k: (k, 0)),
        out_shape=jax.ShapeDtypeStruct((1024, HD), BF),
        compiler_params=params(60),
        cost_estimate=cost(2 * PAIR * D * RANK, 5 * MIB),
        name="down_part",
    )(place, rank, pair)


def finish_kernel(pieces, _, out):
    total = jnp.sum(pieces[...].astype(F32).reshape(128, 8, HD), axis=0)
    for i in range(4):
        out[8 * i : 8 * i + 8, :] = total[:, 32 * i : 32 * i + 32]


def finish(pieces, after):
    return pl.pallas_call(
        finish_kernel,
        in_specs=[whole((1024, HD)), any_ref()],
        out_specs=whole((RANK, 32)),
        out_shape=jax.ShapeDtypeStruct((RANK, 32), F32),
        compiler_params=params(60),
        cost_estimate=cost(MIB, MIB),
        name="finish",
    )(pieces, after)


def join_kernel(place, rank, mine_a, theirs_a, mine_b, theirs_b, factor, out, one, two, result, sems, out_sem):
    half = D // 2
    count = half // CHUNK
    chunks = []
    for i in range(2 * count):
        own, other = (mine_a, theirs_a) if i < count else (mine_b, theirs_b)
        here = pl.ds(i * CHUNK, CHUNK)
        there = pl.ds(i % count * CHUNK, CHUNK)
        chunks.append(
            start_all(
                [
                    pltpu.make_async_copy(own.at[:, there], one.at[:, here], sems.at[0, i]),
                    pltpu.make_async_copy(other.at[:, there], two.at[:, here], sems.at[1, i]),
                ]
            )
        )
    mine = rank[pl.ds(pl.multiple_of(place[1] * 128, 128), 128), :]
    leaving = []
    for i, chunk in enumerate(chunks):
        here = slice(i * CHUNK, (i + 1) * CHUNK)
        adapter = SCALE * jnp.dot(mine, factor[:, here], preferred_element_type=F32)
        wait_all(chunk)
        result[:, here] = (one[:, here].astype(F32) + two[:, here].astype(F32) + adapter).astype(BF)
        cols = pl.ds(i * CHUNK, CHUNK)
        leaving += start_all([pltpu.make_async_copy(result.at[:, cols], out.at[:, cols], out_sem.at[i])])
    wait_all(leaving)


def join(place, rank, mine_a, theirs_a, mine_b, theirs_b, factor):
    return pl.pallas_call(
        join_kernel,
        in_specs=[smem(), whole((PAIR, RANK))] + [any_ref()] * 4 + [whole((RANK, D))],
        out_specs=any_ref(),
        out_shape=jax.ShapeDtypeStruct((128, D), BF),
        scratch_shapes=[pltpu.VMEM((128, D), BF)] * 3
        + [pltpu.SemaphoreType.DMA((2, D // CHUNK)), pltpu.SemaphoreType.DMA((D // CHUNK,))],
        compiler_params=params(60),
        cost_estimate=cost(MIB, MIB),
        name="join",
    )(place, rank, mine_a, theirs_a, mine_b, theirs_b, factor)


def along_z(value, shift):
    return lax.ppermute(value, ("zh", "zl"), [(i, (i + shift) % 8) for i in range(8)])


def to_all(value, axis):
    return lax.all_to_all(jnp.broadcast_to(value[None], (4,) + value.shape), axis, 0, 0, tiled=True)


def gather_weights(w_key, w_val, up):
    place = lax.axis_index("x") * 4 + lax.axis_index("y")
    near, cross = NEAR // 16, CROSS // 16

    def rows(start, count):
        return [lax.dynamic_slice(w, (start, 0), (count, HD)) for w in (w_key, w_val)]

    seed = jnp.concatenate(
        [jnp.concatenate(rows(place * near, near), 1), jnp.concatenate(rows(NEAR + place * cross, cross), 1)], 0
    )
    half = (near + cross) // 2
    first = along_z(seed, -1)
    third = along_z(seed, 1)
    second = jnp.concatenate([along_z(seed[:half], -2), along_z(seed[half:], 2)], axis=0)
    seeds = jnp.concatenate([first, second, third], axis=1)
    far = lax.all_gather(seeds[:near], ("x", "y"), axis=0, tiled=True)
    cross_rows = to_all(to_all(seeds[near:], "y").reshape(4 * cross, 768), "x").reshape(CROSS, 768)
    base = NEAR + CROSS
    own = jnp.concatenate([w_key[base:], w_val[base:]], axis=1)
    own = jnp.concatenate([jnp.pad(up, ((0, 0), (0, HD))), own], axis=0) + seeds[:1, :1] * 0
    one = along_z(own, -1)
    three = along_z(own, 1)
    two_a = along_z(one[: RANK + LINE // 2], -1)
    two_b = along_z(three[RANK + LINE // 2 :], 1)
    ups = jnp.stack([up] + [got[:RANK, :HD] for got in (one, two_a, three)])
    return far, cross_rows, (one, two_a, two_b, three), ups


def shards(hidden, w_key, w_val, factor, up, mag, queries, grad_attn):
    zl, core = lax.axis_index("zl"), lax.axis_index("core")
    place = jnp.stack([zl, core]).astype(jnp.int32)
    swap = [(0, 1), (1, 0)]
    far, cross, line, ups = gather_weights(w_key, w_val, up)
    other = lax.ppermute(hidden, "core", swap)
    pair = jnp.where(
        core == 0, jnp.concatenate([hidden, other], axis=0), jnp.concatenate([other, hidden], axis=0)
    )
    down = lax.dot_general(pair, factor, NT, preferred_element_type=F32).astype(BF)
    all_down = lax.all_to_all(
        jnp.broadcast_to(down[None], (4, PAIR, RANK)), "zl", 0, 0, tiled=True
    ).reshape(SEQ, RANK)
    merged = w_val.astype(F32) + SCALE * lax.dot_general(factor, up, TN, preferred_element_type=F32)
    norms = jnp.sqrt(jnp.sum(merged * merged, axis=0))
    col_scale = (mag / norms).reshape(1, HD)
    cos, sin = rope_tables()
    cos_here = lax.dynamic_slice(cos, (zl * PAIR, 0), (PAIR, HD))
    sin_here = lax.dynamic_slice(sin, (zl * PAIR, 0), (PAIR, HD))
    so_far = project_line(pair, w_key, w_val, cross, line)
    rows = project(place, pair, w_key, w_val, far, so_far, down, ups, cos_here, sin_here)
    rows = lax.all_to_all(rows, "zl", 0, 0, tiled=True).reshape(SEQ, 3 * HD)
    grads, up_grad, mag_grad = attend(queries, grad_attn, rows, col_scale, all_down, cos, sin)
    grads = lax.all_to_all(grads.reshape(4, PAIR, 2 * HD), "zl", 0, 0, tiled=True)
    small = jnp.concatenate([up_grad, mag_grad / norms], axis=0)
    small = small + lax.ppermute(small, "zh", swap)
    small = lax.all_gather(jnp.pad(small, ((0, 88), (0, 0))), ("x", "y"), axis=0, tiled=True)
    small = jnp.sum(small.reshape(16, HD, HD)[:, :40], axis=0)
    part = rank_part(place, grads, ups)
    rank = (part + lax.ppermute(part, "core", swap)).astype(BF)
    pieces = down_part(place, rank, pair)
    mine_a, theirs_a = back(back_near_kernel, [(3, 4)], "back_near", place, grads, w_key, w_val, (far,), pieces)
    theirs_a = lax.ppermute(theirs_a, "core", swap)
    mine_b, theirs_b = back(
        back_line_kernel, [(3, 2), (5, 2)], "back_line", place, grads, w_key, w_val, (cross,) + line, pieces
    )
    theirs_b = lax.ppermute(theirs_b, "core", swap)
    pieces = lax.all_to_all(pieces, DP + ("zl",), 0, 0, tiled=True)
    grad_hidden = join(place, rank, mine_a, theirs_a, mine_b, theirs_b, factor)
    grad_down = finish(pieces, grad_hidden)
    return grad_hidden, grad_down, small[:RANK], small[RANK]


def solution(mesh):
    fine = Mesh(np.asarray(mesh.devices).reshape(4, 4, 2, 4, 2), EVERY)
    tensor = ("zl", "core")
    return jax.shard_map(
        shards,
        mesh=fine,
        in_specs=(
            P(EVERY, None),
            P(None, tensor),
            P(None, tensor),
            P(),
            P(None, tensor),
            P(tensor),
            P(DP, tensor),
            P(DP, tensor),
        ),
        out_specs=(P(EVERY, None), P(None, EVERY), P(None, tensor), P(tensor)),
        check_vma=False,
    )
```

```python
import jax
import jax.numpy as jnp
import numpy as np
from jax import lax
from jax.experimental import pallas as pl
from jax.experimental.pallas import tpu as pltpu
from jax.sharding import Mesh, PartitionSpec as P

HD = 128
D = 8192
SEQ = 1024
RANK = 32
PAIR = 256
NEAR = 4096
CROSS = 2048
LINE = 2048
CHUNK = 1024
QB = 256
GROUP = 4
SCALE = 2.0
ROPE_BASE = 500000.0
LOG2E = 1.4426950408889634
INV_SQRT = HD ** (-0.5)
MIB = 1024 * 1024
BF = jnp.bfloat16
F32 = jnp.float32
NT = (((1,), (1,)), ((), ()))
TN = (((0,), (0,)), ((), ()))
EVERY = ("x", "y", "zh", "zl", "core")
DP = ("x", "y", "zh")


def rope_tables():
    half = HD // 2
    frequency = ROPE_BASE ** (-(jnp.arange(half, dtype=F32) * 2.0 / HD))
    angles = jnp.arange(SEQ, dtype=F32)[:, None] * frequency[None, :]
    cosine, sine = jnp.cos(angles), jnp.sin(angles)
    return jnp.concatenate([cosine, cosine], 1), jnp.concatenate([-sine, sine], 1)


def smem():
    return pl.BlockSpec(memory_space=pltpu.SMEM)


def whole(shape):
    return pl.BlockSpec(shape, lambda *_: (0,) * len(shape))


def params(limit):
    return pltpu.CompilerParams(vmem_limit_bytes=limit * MIB)


def cost(flops, moved, trans=0):
    return pl.CostEstimate(flops=flops, bytes_accessed=moved, transcendentals=trans)


def any_ref():
    return pl.BlockSpec(memory_space=pl.ANY)


def start_all(copies):
    for copy in copies:
        copy.start()
    return copies


def wait_all(copies):
    for copy in copies:
        copy.wait()


def near_copies(base, first, own_key, own_val, far, weights, sems):
    chunks = []
    for i in range(far.shape[0] // CHUNK):
        here = pl.ds(first + i * CHUNK, CHUNK)
        near = pl.ds(i * CHUNK, CHUNK)
        there = pl.ds(base + i * CHUNK, CHUNK)
        chunks.append(
            [
                pltpu.make_async_copy(own_key.at[there, :], weights.at[here, pl.ds(0, HD)], sems.at[0, i]),
                pltpu.make_async_copy(own_val.at[there, :], weights.at[here, pl.ds(HD, HD)], sems.at[1, i]),
                pltpu.make_async_copy(far.at[near, :], weights.at[here, pl.ds(256, 768)], sems.at[2, i]),
            ]
        )
    return chunks


def line_copies(base, first, own_key, own_val, one, two_a, two_b, three, weights, sems):
    chunks = []
    size = LINE // 2
    for i, two in enumerate((two_a.at[pl.ds(RANK, size), :], two_b)):
        here = pl.ds(first + i * size, size)
        there = pl.ds(base + i * size, size)
        near = pl.ds(RANK + i * size, size)
        chunks.append(
            [
                pltpu.make_async_copy(own_key.at[there, :], weights.at[here, pl.ds(0, HD)], sems.at[0, i]),
                pltpu.make_async_copy(own_val.at[there, :], weights.at[here, pl.ds(HD, HD)], sems.at[1, i]),
                pltpu.make_async_copy(one.at[near, :], weights.at[here, pl.ds(256, 256)], sems.at[2, i]),
                pltpu.make_async_copy(two, weights.at[here, pl.ds(512, 256)], sems.at[3, i]),
                pltpu.make_async_copy(three.at[near, :], weights.at[here, pl.ds(768, 256)], sems.at[4, i]),
            ]
        )
    return chunks


def pair_copies(pair, hid, base, count, sem):
    size = hid.shape[1] // count
    return [
        pltpu.make_async_copy(
            pair.at[:, pl.ds(base + i * size, size)], hid.at[:, pl.ds(i * size, size)], sem.at[i]
        )
        for i in range(count)
    ]


def multiply(acc, chunks, hid_chunks, hid, weights):
    size = hid.shape[1] // len(chunks)
    for i, chunk in enumerate(chunks):
        wait_all(chunk + [hid_chunks[i]])
        here = slice(i * size, (i + 1) * size)
        term = jnp.dot(hid[:, here], weights[here, :], preferred_element_type=F32)
        acc = term if acc is None else acc + term
    return acc


def project_line_kernel(
    pair, own_key, own_val, cross, one, two_a, two_b, three, out, hid, weights, hid_sem, sems, line_sems
):
    chunks = near_copies(NEAR, 0, own_key, own_val, cross, weights, sems)
    chunks += line_copies(
        NEAR + CROSS, CROSS, own_key, own_val, one, two_a, two_b, three, weights, line_sems
    )
    hid_chunks = pair_copies(pair, hid, NEAR, 4, hid_sem)
    for i in range(4):
        start_all(chunks[i] + [hid_chunks[i]])
    out[...] = multiply(None, chunks, hid_chunks, hid, weights)


def project_line(pair, w_key, w_val, cross, line):
    return pl.pallas_call(
        project_line_kernel,
        in_specs=[any_ref()] * 8,
        out_specs=whole((PAIR, 1024)),
        out_shape=jax.ShapeDtypeStruct((PAIR, 1024), F32),
        scratch_shapes=[
            pltpu.VMEM((PAIR, CROSS + LINE), BF),
            pltpu.VMEM((CROSS + LINE, 1024), BF),
            pltpu.SemaphoreType.DMA((4,)),
            pltpu.SemaphoreType.DMA((3, 2)),
            pltpu.SemaphoreType.DMA((5, 2)),
        ],
        compiler_params=params(60),
        cost_estimate=cost(2 * PAIR * (CROSS + LINE) * 1024, 11 * MIB),
        name="project_line",
    )(pair, w_key, w_val, cross, *line)


def project_kernel(
    place, pair, own_key, own_val, far, so_far, down, ups, cos, sin, out, hid, weights, hid_sem, sems
):
    count = NEAR // CHUNK
    chunks = near_copies(0, 0, own_key, own_val, far, weights, sems)
    hid_chunks = pair_copies(pair, hid, 0, count, hid_sem)
    for i in range(count):
        start_all(chunks[i] + [hid_chunks[i]])
    acc = multiply(so_far[...], chunks, hid_chunks, hid, weights)
    packed = jnp.concatenate([down[64 * j : 64 * j + 64, :] for j in range(4)], axis=1)
    packed = jnp.concatenate([packed[:32], packed[32:], jnp.zeros((32, HD), BF)], axis=1)
    for r in range(4):
        key = acc[:, r * 256 : r * 256 + HD]
        turned = key * cos[...] + pltpu.roll(key, HD // 2, 1) * sin[...]
        turned = turned * (INV_SQRT * LOG2E)
        high = turned.astype(BF)
        low = (turned - high.astype(F32)).astype(BF)
        lifted = jnp.dot(down[...], ups[r], preferred_element_type=F32)
        base = (acc[:, r * 256 + HD : (r + 1) * 256] + SCALE * lifted).astype(BF)
        slot = lax.rem(place[0] + r, 4)
        out[slot, :PAIR, :] = jnp.concatenate([high, low, base], axis=1)
        out[slot, PAIR:, :] = packed


def project(place, pair, w_key, w_val, far, so_far, down, ups, cos, sin):
    count = NEAR // CHUNK
    return pl.pallas_call(
        project_kernel,
        in_specs=[
            smem(),
            any_ref(),
            any_ref(),
            any_ref(),
            any_ref(),
            whole((PAIR, 1024)),
            whole((PAIR, RANK)),
            whole((4, RANK, HD)),
            whole((PAIR, HD)),
            whole((PAIR, HD)),
        ],
        out_specs=whole((4, PAIR + 32, 3 * HD)),
        out_shape=jax.ShapeDtypeStruct((4, PAIR + 32, 3 * HD), BF),
        scratch_shapes=[
            pltpu.VMEM((PAIR, NEAR), BF),
            pltpu.VMEM((NEAR, 1024), BF),
            pltpu.SemaphoreType.DMA((count,)),
            pltpu.SemaphoreType.DMA((3, count)),
        ],
        compiler_params=params(60),
        cost_estimate=cost(2 * PAIR * NEAR * 1024, 14 * MIB),
        name="project",
    )(place, pair, w_key, w_val, far, so_far, down, ups, cos, sin)


def attend_kernel(query, grad, rows, col_scale, cos, sin, grads, up_grad, mag_grad, keys, vals, dkey, dval):
    head = pl.program_id(0)

    @pl.when(head == 0)
    def _():
        for i in range(4):
            here = slice(i * PAIR, (i + 1) * PAIR)
            keys[here, :] = rows[i, :PAIR, : 2 * HD]
            vals[here, :] = (rows[i, :PAIR, 2 * HD :].astype(F32) * col_scale[...]).astype(BF)
        dkey[...] = jnp.zeros_like(dkey)
        dval[...] = jnp.zeros_like(dval)

    for block in range(SEQ // QB):
        stop = (block + 1) * QB
        here = slice(block * QB, stop)
        q = query[here, :]
        g = grad[here, :]
        qq = jnp.concatenate([q, q], axis=1)
        scores = lax.dot_general(keys[:stop], qq, NT, preferred_element_type=F32)
        key_at = lax.broadcasted_iota(jnp.int32, (QB, QB), 0)
        query_at = lax.broadcasted_iota(jnp.int32, (QB, QB), 1)
        edge = jnp.where(key_at <= query_at, scores[block * QB :], -1e30)
        if block:
            scores = jnp.concatenate([scores[: block * QB], edge], axis=0)
        else:
            scores = edge
        powers = jnp.exp2(scores - jnp.max(scores, axis=0, keepdims=True))
        attn = powers * (1.0 / jnp.sum(powers, axis=0, keepdims=True))
        half = attn.astype(BF)
        pgrad = lax.dot_general(vals[:stop], g, NT, preferred_element_type=F32)
        delta = jnp.sum(half.astype(F32) * pgrad, axis=0, keepdims=True)
        sgrad = (attn * (pgrad - delta)).astype(BF)
        dval[:stop] += jnp.dot(half, g, preferred_element_type=F32)
        dkey[:stop] += jnp.dot(sgrad, q, preferred_element_type=F32)

    @pl.when(head == pl.num_programs(0) - 1)
    def _():
        dk = dkey[...] * INV_SQRT
        dk = dk * cos[...] - pltpu.roll(dk, HD // 2, 1) * sin[...]
        dv = dval[...]
        gv = (dv * col_scale[...]).astype(BF)
        grads[:, :HD] = dk.astype(BF)
        grads[:, HD:] = gv
        total = jnp.zeros((RANK, HD), F32)
        mags = jnp.zeros((1, HD), F32)
        for i in range(4):
            here = slice(i * PAIR, (i + 1) * PAIR)
            packed = rows[i, PAIR:, : 2 * HD]
            packed = jnp.concatenate([packed[:, :HD], packed[:, HD:]], axis=0)
            down = jnp.concatenate([packed[:, 32 * j : 32 * j + 32] for j in range(4)], axis=0)
            total += lax.dot_general(down, gv[here], TN, preferred_element_type=F32)
            mags += jnp.sum(dv[here] * rows[i, :PAIR, 2 * HD :].astype(F32), axis=0, keepdims=True)
        up_grad[...] = SCALE * total
        mag_grad[...] = jnp.broadcast_to(mags, mag_grad.shape)


def attend(queries, grad_attn, rows, col_scale, cos, sin):
    return pl.pallas_call(
        attend_kernel,
        grid=(GROUP,),
        in_specs=[
            pl.BlockSpec((SEQ, HD), lambda h: (0, h)),
            pl.BlockSpec((SEQ, HD), lambda h: (0, h)),
            whole((4, PAIR + 32, 3 * HD)),
            whole((1, HD)),
            whole((SEQ, HD)),
            whole((SEQ, HD)),
        ],
        out_specs=[whole((SEQ, 2 * HD)), whole((RANK, HD)), whole((8, HD))],
        out_shape=[
            jax.ShapeDtypeStruct((SEQ, 2 * HD), BF),
            jax.ShapeDtypeStruct((RANK, HD), F32),
            jax.ShapeDtypeStruct((8, HD), F32),
        ],
        scratch_shapes=[
            pltpu.VMEM((SEQ, 2 * HD), BF),
            pltpu.VMEM((SEQ, HD), BF),
            pltpu.VMEM((SEQ, HD), F32),
            pltpu.VMEM((SEQ, HD), F32),
        ],
        compiler_params=params(60),
        cost_estimate=cost(5 * 2 * GROUP * SEQ * SEQ * HD, 6 * MIB, GROUP * SEQ * SEQ),
        name="attend",
    )(queries, grad_attn, rows, col_scale, cos, sin)


def rank_kernel(place, grads, ups, out):
    total = jnp.zeros((PAIR, RANK), F32)
    for r in range(4):
        slot = lax.rem(place[0] + r, 4)
        total += lax.dot_general(grads[slot, :, HD:], ups[r], NT, preferred_element_type=F32)
    out[...] = total


def rank_part(place, grads, ups):
    return pl.pallas_call(
        rank_kernel,
        in_specs=[smem(), whole((4, PAIR, 2 * HD)), whole((4, RANK, HD))],
        out_specs=whole((PAIR, RANK)),
        out_shape=jax.ShapeDtypeStruct((PAIR, RANK), F32),
        compiler_params=params(60),
        cost_estimate=cost(2 * PAIR * 512 * RANK, MIB),
        name="rank_part",
    )(place, grads, ups)


def spread(place, grads, start, left):
    for r in range(4):
        slot = lax.rem(place[0] + r, 4)
        left[:, r * 256 : (r + 1) * 256] = grads[slot, pl.ds(pl.multiple_of(start, 128), 128), :]


def weight_copies(own_key, own_val, far, cross, one, two_a, two_b, three, weights, far_sems, cross_sems, line_sems):
    chunks = near_copies(0, 0, own_key, own_val, far, weights, far_sems)
    chunks += near_copies(NEAR, NEAR, own_key, own_val, cross, weights, cross_sems)
    base = NEAR + CROSS
    chunks += line_copies(base, base, own_key, own_val, one, two_a, two_b, three, weights, line_sems)
    return chunks


def weight_scratch():
    return [
        pltpu.VMEM((128, 1024), BF),
        pltpu.VMEM((D, 1024), BF),
        pltpu.SemaphoreType.DMA((3, NEAR // CHUNK)),
        pltpu.SemaphoreType.DMA((3, CROSS // CHUNK)),
        pltpu.SemaphoreType.DMA((5, 2)),
    ]


def back_theirs_kernel(
    place, grads, own_key, own_val, far, cross, one, two_a, two_b, three, _, out,
    left, weights, far_sems, cross_sems, line_sems, part, out_sem,
):
    chunks = weight_copies(
        own_key, own_val, far, cross, one, two_a, two_b, three, weights, far_sems, cross_sems, line_sems
    )
    for chunk in chunks:
        start_all(chunk)
    spread(place, grads, 128 - place[1] * 128, left)
    leaving = []
    for i, chunk in enumerate(chunks):
        wait_all(chunk)
        here = slice(i * CHUNK, (i + 1) * CHUNK)
        part[:, here] = lax.dot_general(left[...], weights[here, :], NT, preferred_element_type=F32).astype(BF)
        cols = pl.ds(i * CHUNK, CHUNK)
        leaving += start_all([pltpu.make_async_copy(part.at[:, cols], out.at[:, cols], out_sem.at[i])])
    wait_all(leaving)


def back_theirs(place, grads, all_weights, *after):
    return pl.pallas_call(
        back_theirs_kernel,
        in_specs=[smem(), whole((4, PAIR, 2 * HD))] + [any_ref()] * 9,
        out_specs=any_ref(),
        out_shape=jax.ShapeDtypeStruct((128, D), BF),
        scratch_shapes=weight_scratch() + [pltpu.VMEM((128, D), BF), pltpu.SemaphoreType.DMA((D // CHUNK,))],
        compiler_params=params(60),
        cost_estimate=cost(2 * 128 * D * 1024, 18 * MIB),
        name="back_theirs",
    )(place, grads, *all_weights, *after)


def back_mine_kernel(
    place, grads, rank, factor, theirs, own_key, own_val, far, cross, one, two_a, two_b, three, out,
    left, weights, far_sems, cross_sems, line_sems, other, part, other_sem, out_sem,
):
    chunks = weight_copies(
        own_key, own_val, far, cross, one, two_a, two_b, three, weights, far_sems, cross_sems, line_sems
    )
    for i, chunk in enumerate(chunks):
        cols = pl.ds(i * CHUNK, CHUNK)
        chunk.append(pltpu.make_async_copy(theirs.at[:, cols], other.at[:, cols], other_sem.at[i]))
        start_all(chunk)
    start = pl.multiple_of(place[1] * 128, 128)
    spread(place, grads, start, left)
    mine = rank[pl.ds(start, 128), :]
    leaving = []
    for i, chunk in enumerate(chunks):
        here = slice(i * CHUNK, (i + 1) * CHUNK)
        adapter = SCALE * jnp.dot(mine, factor[:, here], preferred_element_type=F32)
        wait_all(chunk)
        term = lax.dot_general(left[...], weights[here, :], NT, preferred_element_type=F32)
        part[:, here] = (term + other[:, here].astype(F32) + adapter).astype(BF)
        cols = pl.ds(i * CHUNK, CHUNK)
        leaving += start_all([pltpu.make_async_copy(part.at[:, cols], out.at[:, cols], out_sem.at[i])])
    wait_all(leaving)


def back_mine(place, grads, rank, factor, theirs, all_weights):
    return pl.pallas_call(
        back_mine_kernel,
        in_specs=[smem(), whole((4, PAIR, 2 * HD)), whole((PAIR, RANK)), whole((RANK, D))] + [any_ref()] * 9,
        out_specs=any_ref(),
        out_shape=jax.ShapeDtypeStruct((128, D), BF),
        scratch_shapes=weight_scratch()
        + [pltpu.VMEM((128, D), BF)] * 2
        + [pltpu.SemaphoreType.DMA((D // CHUNK,))] * 2,
        compiler_params=params(60),
        cost_estimate=cost(2 * 128 * D * 1024, 20 * MIB),
        name="back_mine",
    )(place, grads, rank, factor, theirs, *all_weights)


def down_kernel(place, rank, hid, _, out):
    part = SCALE * lax.dot_general(rank[...], hid[...], TN, preferred_element_type=F32)
    lane = lax.broadcasted_iota(jnp.int32, (8, HD), 1) // 32
    core = place[1]
    for tile in range(part.shape[1] // HD):
        regs = [part[8 * i : 8 * i + 8, tile * HD : (tile + 1) * HD] for i in range(4)]
        blocks = []
        for pick in range(2):
            column = 2 * pick + core
            block = jnp.zeros((8, HD), F32)
            for i in range(4):
                moved = pltpu.roll(regs[i], lax.rem((i - column + 4) * 32, HD), 1)
                block = jnp.where(lane == i, moved, block)
            blocks.append(block)
        out[16 * tile : 16 * tile + 16, :] = jnp.concatenate(blocks, axis=0).astype(BF)


def down_part(place, rank, pair, after):
    wide = 2048
    return pl.pallas_call(
        down_kernel,
        grid=(D // wide,),
        in_specs=[smem(), whole((PAIR, RANK)), pl.BlockSpec((PAIR, wide), lambda k: (0, k)), any_ref()],
        out_specs=pl.BlockSpec((wide // 8, HD), lambda k: (k, 0)),
        out_shape=jax.ShapeDtypeStruct((1024, HD), BF),
        compiler_params=params(60),
        cost_estimate=cost(2 * PAIR * D * RANK, 5 * MIB),
        name="down_part",
    )(place, rank, pair, after)


def finish_kernel(pieces, _, out):
    total = jnp.sum(pieces[...].astype(F32).reshape(128, 8, HD), axis=0)
    for i in range(4):
        out[8 * i : 8 * i + 8, :] = total[:, 32 * i : 32 * i + 32]


def finish(pieces, after):
    return pl.pallas_call(
        finish_kernel,
        in_specs=[whole((1024, HD)), any_ref()],
        out_specs=whole((RANK, 32)),
        out_shape=jax.ShapeDtypeStruct((RANK, 32), F32),
        compiler_params=params(60),
        cost_estimate=cost(0, 0),
        name="finish",
    )(pieces, after)


def ordered_kernel(me, *refs):
    slots = refs[-1]
    for s in range(4):
        slots[lax.rem(me[0] + s, 4)] = refs[s][...]
    refs[4][...] = slots[0] + slots[1] + slots[2] + slots[3]


def sum_four(value, axis):
    me = lax.axis_index(axis).astype(jnp.int32).reshape(1)
    parts = [value] + [lax.ppermute(value, axis, [(i, (i - s) % 4) for i in range(4)]) for s in (1, 2, 3)]
    return pl.pallas_call(
        ordered_kernel,
        in_specs=[smem()] + [whole(value.shape)] * 4,
        out_specs=whole(value.shape),
        out_shape=jax.ShapeDtypeStruct(value.shape, F32),
        scratch_shapes=[pltpu.VMEM((4,) + value.shape, F32)],
        compiler_params=params(60),
        cost_estimate=cost(0, 0),
        name="sum_four",
    )(me, *parts)


def along_z(value, shift):
    return lax.ppermute(value, ("zh", "zl"), [(i, (i + shift) % 8) for i in range(8)])


def to_all(value, axis):
    return lax.all_to_all(jnp.broadcast_to(value[None], (4,) + value.shape), axis, 0, 0, tiled=True)


def gather_weights(w_key, w_val, up):
    place = lax.axis_index("x") * 4 + lax.axis_index("y")
    turned = lax.axis_index("y") * 4 + lax.axis_index("x")
    near, cross = NEAR // 16, CROSS // 16

    def rows(start, count):
        return [lax.dynamic_slice(w, (start, 0), (count, HD)) for w in (w_key, w_val)]

    seed = jnp.concatenate(
        [jnp.concatenate(rows(place * near, near), 1), jnp.concatenate(rows(NEAR + turned * cross, cross), 1)], 0
    )
    half = (near + cross) // 2
    first = along_z(seed, -1)
    third = along_z(seed, 1)
    second = jnp.concatenate([along_z(seed[:half], -2), along_z(seed[half:], 2)], axis=0)
    seeds = jnp.concatenate([first, second, third], axis=1)
    far = lax.all_gather(seeds[:near], ("x", "y"), axis=0, tiled=True)
    cross_rows = to_all(to_all(seeds[near:], "x").reshape(4 * cross, 768), "y").reshape(CROSS, 768)
    base = NEAR + CROSS
    own = jnp.concatenate([w_key[base:], w_val[base:]], axis=1)
    own = jnp.concatenate([jnp.pad(up, ((0, 0), (0, HD))), own], axis=0) + seeds[:1, :1] * 0
    one = along_z(own, -1)
    three = along_z(own, 1)
    two_a = along_z(one[: RANK + LINE // 2], -1)
    two_b = along_z(three[RANK + LINE // 2 :], 1)
    ups = jnp.stack([up] + [got[:RANK, :HD] for got in (one, two_a, three)])
    return far, cross_rows, (one, two_a, two_b, three), ups


def shards(hidden, w_key, w_val, factor, up, mag, queries, grad_attn):
    zl, core = lax.axis_index("zl"), lax.axis_index("core")
    place = jnp.stack([zl, core]).astype(jnp.int32)
    swap = [(0, 1), (1, 0)]
    other = lax.ppermute(hidden, "core", swap)
    pair = jnp.where(
        core == 0, jnp.concatenate([hidden, other], axis=0), jnp.concatenate([other, hidden], axis=0)
    )
    down = lax.dot_general(pair, factor, NT, preferred_element_type=F32).astype(BF)
    far, cross, line, ups = gather_weights(w_key, w_val, up)
    merged = w_val.astype(F32) + SCALE * lax.dot_general(factor, up, TN, preferred_element_type=F32)
    norms = jnp.sqrt(jnp.sum(merged * merged, axis=0))
    col_scale = (mag / norms).reshape(1, HD)
    cos, sin = rope_tables()
    cos_here = lax.dynamic_slice(cos, (zl * PAIR, 0), (PAIR, HD))
    sin_here = lax.dynamic_slice(sin, (zl * PAIR, 0), (PAIR, HD))
    so_far = project_line(pair, w_key, w_val, cross, line)
    rows = project(place, pair, w_key, w_val, far, so_far, down, ups, cos_here, sin_here)
    rows = lax.all_to_all(rows, "zl", 0, 0, tiled=True)
    grads, up_grad, mag_grad = attend(queries, grad_attn, rows, col_scale, cos, sin)
    grads = lax.all_to_all(grads.reshape(4, PAIR, 2 * HD), "zl", 0, 0, tiled=True)
    small = jnp.concatenate([up_grad, mag_grad / norms], axis=0)
    small = small + lax.ppermute(small, "zh", swap)
    all_weights = (w_key, w_val, far, cross) + line
    part = rank_part(place, grads, ups)
    theirs = lax.ppermute(back_theirs(place, grads, all_weights, small), "core", swap)
    rank = (part + lax.ppermute(part, "core", swap)).astype(BF)
    small = sum_four(small, "x")
    pieces = lax.all_to_all(down_part(place, rank, pair, small), DP + ("zl",), 0, 0, tiled=True)
    grad_hidden = back_mine(place, grads, rank, factor, theirs, all_weights)
    small = sum_four(small, "y")
    return grad_hidden, finish(pieces, grad_hidden), small[:RANK], small[RANK]


def solution(mesh):
    fine = Mesh(np.asarray(mesh.devices).reshape(4, 4, 2, 4, 2), EVERY)
    tensor = ("zl", "core")
    return jax.shard_map(
        shards,
        mesh=fine,
        in_specs=(
            P(EVERY, None),
            P(None, tensor),
            P(None, tensor),
            P(),
            P(None, tensor),
            P(tensor),
            P(DP, tensor),
            P(DP, tensor),
        ),
        out_specs=(P(EVERY, None), P(None, EVERY), P(None, tensor), P(tensor)),
        check_vma=False,
    )
```

```python
import jax
import jax.numpy as jnp
import numpy as np
from jax import lax
from jax.experimental import pallas as pl
from jax.experimental.pallas import tpu as pltpu
from jax.sharding import Mesh, PartitionSpec as P

HD = 128
D = 8192
SEQ = 1024
RANK = 32
PAIR = 256
NEAR = 5120
LINE = 3072
CHUNK = 1280
QB = 256
GROUP = 4
SCALE = 2.0
ROPE_BASE = 500000.0
LOG2E = 1.4426950408889634
INV_SQRT = HD ** (-0.5)
MIB = 1024 * 1024
BF = jnp.bfloat16
F32 = jnp.float32
NT = (((1,), (1,)), ((), ()))
TN = (((0,), (0,)), ((), ()))
EVERY = ("x", "y", "zh", "zl", "core")
DP = ("x", "y", "zh")


def rope_tables():
    half = HD // 2
    frequency = ROPE_BASE ** (-(jnp.arange(half, dtype=F32) * 2.0 / HD))
    angles = jnp.arange(SEQ, dtype=F32)[:, None] * frequency[None, :]
    cosine, sine = jnp.cos(angles), jnp.sin(angles)
    return jnp.concatenate([cosine, cosine], 1), jnp.concatenate([-sine, sine], 1)


def smem():
    return pl.BlockSpec(memory_space=pltpu.SMEM)


def whole(shape):
    return pl.BlockSpec(shape, lambda *_: (0,) * len(shape))


def params(limit):
    return pltpu.CompilerParams(vmem_limit_bytes=limit * MIB)


def cost(flops, moved, trans=0):
    return pl.CostEstimate(flops=flops, bytes_accessed=moved, transcendentals=trans)


def any_ref():
    return pl.BlockSpec(memory_space=pl.ANY)


def start_all(copies):
    for copy in copies:
        copy.start()
    return copies


def wait_all(copies):
    for copy in copies:
        copy.wait()


def near_copies(base, first, own_key, own_val, far, weights, sems):
    chunks = []
    for i in range(far.shape[0] // CHUNK):
        here = pl.ds(first + i * CHUNK, CHUNK)
        near = pl.ds(i * CHUNK, CHUNK)
        there = pl.ds(base + i * CHUNK, CHUNK)
        chunks.append(
            [
                pltpu.make_async_copy(own_key.at[there, :], weights.at[here, pl.ds(0, HD)], sems.at[0, i]),
                pltpu.make_async_copy(own_val.at[there, :], weights.at[here, pl.ds(HD, HD)], sems.at[1, i]),
                pltpu.make_async_copy(far.at[near, :], weights.at[here, pl.ds(256, 768)], sems.at[2, i]),
            ]
        )
    return chunks


def line_copies(base, first, own_key, own_val, one, two_a, two_b, three, weights, sems):
    chunks = []
    size = LINE // 2
    for i, two in enumerate((two_a.at[pl.ds(RANK, size), :], two_b)):
        here = pl.ds(first + i * size, size)
        there = pl.ds(base + i * size, size)
        near = pl.ds(RANK + i * size, size)
        chunks.append(
            [
                pltpu.make_async_copy(own_key.at[there, :], weights.at[here, pl.ds(0, HD)], sems.at[0, i]),
                pltpu.make_async_copy(own_val.at[there, :], weights.at[here, pl.ds(HD, HD)], sems.at[1, i]),
                pltpu.make_async_copy(one.at[near, :], weights.at[here, pl.ds(256, 256)], sems.at[2, i]),
                pltpu.make_async_copy(two, weights.at[here, pl.ds(512, 256)], sems.at[3, i]),
                pltpu.make_async_copy(three.at[near, :], weights.at[here, pl.ds(768, 256)], sems.at[4, i]),
            ]
        )
    return chunks


def pair_copies(pair, hid, base, count, sem):
    size = hid.shape[1] // count
    return [
        pltpu.make_async_copy(
            pair.at[:, pl.ds(base + i * size, size)], hid.at[:, pl.ds(i * size, size)], sem.at[i]
        )
        for i in range(count)
    ]


def multiply(acc, chunks, hid_chunks, hid, weights):
    size = hid.shape[1] // len(chunks)
    for i, chunk in enumerate(chunks):
        wait_all(chunk + [hid_chunks[i]])
        here = slice(i * size, (i + 1) * size)
        term = jnp.dot(hid[:, here], weights[here, :], preferred_element_type=F32)
        acc = term if acc is None else acc + term
    return acc


def project_line_kernel(
    pair, own_key, own_val, one, two_a, two_b, three, out, hid, weights, hid_sem, sems
):
    chunks = line_copies(NEAR, 0, own_key, own_val, one, two_a, two_b, three, weights, sems)
    hid_chunks = pair_copies(pair, hid, NEAR, 2, hid_sem)
    for i in range(2):
        start_all(chunks[i] + [hid_chunks[i]])
    out[...] = multiply(None, chunks, hid_chunks, hid, weights)


def project_line(pair, w_key, w_val, line):
    return pl.pallas_call(
        project_line_kernel,
        in_specs=[any_ref()] * 7,
        out_specs=whole((PAIR, 1024)),
        out_shape=jax.ShapeDtypeStruct((PAIR, 1024), F32),
        scratch_shapes=[
            pltpu.VMEM((PAIR, LINE), BF),
            pltpu.VMEM((LINE, 1024), BF),
            pltpu.SemaphoreType.DMA((2,)),
            pltpu.SemaphoreType.DMA((5, 2)),
        ],
        compiler_params=params(60),
        cost_estimate=cost(2 * PAIR * LINE * 1024, 8 * MIB),
        name="project_line",
    )(pair, w_key, w_val, *line)


def project_kernel(
    place, pair, own_key, own_val, far, so_far, down, ups, cos, sin, out, hid, weights, hid_sem, sems
):
    count = NEAR // CHUNK
    chunks = near_copies(0, 0, own_key, own_val, far, weights, sems)
    hid_chunks = pair_copies(pair, hid, 0, count, hid_sem)
    for i in range(count):
        start_all(chunks[i] + [hid_chunks[i]])
    acc = multiply(so_far[...], chunks, hid_chunks, hid, weights)
    packed = jnp.concatenate([down[64 * j : 64 * j + 64, :] for j in range(4)], axis=1)
    packed = jnp.concatenate([packed[:32], packed[32:], jnp.zeros((32, HD), BF)], axis=1)
    for r in range(4):
        key = acc[:, r * 256 : r * 256 + HD]
        turned = key * cos[...] + pltpu.roll(key, HD // 2, 1) * sin[...]
        turned = turned * (INV_SQRT * LOG2E)
        high = turned.astype(BF)
        low = (turned - high.astype(F32)).astype(BF)
        lifted = jnp.dot(down[...], ups[r], preferred_element_type=F32)
        base = (acc[:, r * 256 + HD : (r + 1) * 256] + SCALE * lifted).astype(BF)
        slot = lax.rem(place[0] + r, 4)
        out[slot, :PAIR, :] = jnp.concatenate([high, low, base], axis=1)
        out[slot, PAIR:, :] = packed


def project(place, pair, w_key, w_val, far, so_far, down, ups, cos, sin):
    count = NEAR // CHUNK
    return pl.pallas_call(
        project_kernel,
        in_specs=[
            smem(),
            any_ref(),
            any_ref(),
            any_ref(),
            any_ref(),
            whole((PAIR, 1024)),
            whole((PAIR, RANK)),
            whole((4, RANK, HD)),
            whole((PAIR, HD)),
            whole((PAIR, HD)),
        ],
        out_specs=whole((4, PAIR + 32, 3 * HD)),
        out_shape=jax.ShapeDtypeStruct((4, PAIR + 32, 3 * HD), BF),
        scratch_shapes=[
            pltpu.VMEM((PAIR, NEAR), BF),
            pltpu.VMEM((NEAR, 1024), BF),
            pltpu.SemaphoreType.DMA((count,)),
            pltpu.SemaphoreType.DMA((3, count)),
        ],
        compiler_params=params(60),
        cost_estimate=cost(2 * PAIR * NEAR * 1024, 14 * MIB),
        name="project",
    )(place, pair, w_key, w_val, far, so_far, down, ups, cos, sin)


def attend_kernel(query, grad, rows, col_scale, cos, sin, grads, up_grad, mag_grad, keys, vals, dkey, dval):
    head = pl.program_id(0)

    @pl.when(head == 0)
    def _():
        for i in range(4):
            here = slice(i * PAIR, (i + 1) * PAIR)
            keys[here, :] = rows[i, :PAIR, : 2 * HD]
            vals[here, :] = (rows[i, :PAIR, 2 * HD :].astype(F32) * col_scale[...]).astype(BF)
        dkey[...] = jnp.zeros_like(dkey)
        dval[...] = jnp.zeros_like(dval)

    for block in range(SEQ // QB):
        stop = (block + 1) * QB
        here = slice(block * QB, stop)
        q = query[here, :]
        g = grad[here, :]
        qq = jnp.concatenate([q, q], axis=1)
        scores = lax.dot_general(keys[:stop], qq, NT, preferred_element_type=F32)
        key_at = lax.broadcasted_iota(jnp.int32, (QB, QB), 0)
        query_at = lax.broadcasted_iota(jnp.int32, (QB, QB), 1)
        edge = jnp.where(key_at <= query_at, scores[block * QB :], -1e30)
        if block:
            scores = jnp.concatenate([scores[: block * QB], edge], axis=0)
        else:
            scores = edge
        powers = jnp.exp2(scores - jnp.max(scores, axis=0, keepdims=True))
        attn = powers * (1.0 / jnp.sum(powers, axis=0, keepdims=True))
        half = attn.astype(BF)
        pgrad = lax.dot_general(vals[:stop], g, NT, preferred_element_type=F32)
        delta = jnp.sum(half.astype(F32) * pgrad, axis=0, keepdims=True)
        sgrad = (attn * (pgrad - delta)).astype(BF)
        dval[:stop] += jnp.dot(half, g, preferred_element_type=F32)
        dkey[:stop] += jnp.dot(sgrad, q, preferred_element_type=F32)

    @pl.when(head == pl.num_programs(0) - 1)
    def _():
        dk = dkey[...] * INV_SQRT
        dk = dk * cos[...] - pltpu.roll(dk, HD // 2, 1) * sin[...]
        dv = dval[...]
        gv = (dv * col_scale[...]).astype(BF)
        grads[:, :HD] = dk.astype(BF)
        grads[:, HD:] = gv
        total = jnp.zeros((RANK, HD), F32)
        mags = jnp.zeros((1, HD), F32)
        for i in range(4):
            here = slice(i * PAIR, (i + 1) * PAIR)
            packed = rows[i, PAIR:, : 2 * HD]
            packed = jnp.concatenate([packed[:, :HD], packed[:, HD:]], axis=0)
            down = jnp.concatenate([packed[:, 32 * j : 32 * j + 32] for j in range(4)], axis=0)
            total += lax.dot_general(down, gv[here], TN, preferred_element_type=F32)
            mags += jnp.sum(dv[here] * rows[i, :PAIR, 2 * HD :].astype(F32), axis=0, keepdims=True)
        up_grad[...] = SCALE * total
        mag_grad[...] = jnp.broadcast_to(mags, mag_grad.shape)


def attend(queries, grad_attn, rows, col_scale, cos, sin):
    return pl.pallas_call(
        attend_kernel,
        grid=(GROUP,),
        in_specs=[
            pl.BlockSpec((SEQ, HD), lambda h: (0, h)),
            pl.BlockSpec((SEQ, HD), lambda h: (0, h)),
            whole((4, PAIR + 32, 3 * HD)),
            whole((1, HD)),
            whole((SEQ, HD)),
            whole((SEQ, HD)),
        ],
        out_specs=[whole((SEQ, 2 * HD)), whole((RANK, HD)), whole((8, HD))],
        out_shape=[
            jax.ShapeDtypeStruct((SEQ, 2 * HD), BF),
            jax.ShapeDtypeStruct((RANK, HD), F32),
            jax.ShapeDtypeStruct((8, HD), F32),
        ],
        scratch_shapes=[
            pltpu.VMEM((SEQ, 2 * HD), BF),
            pltpu.VMEM((SEQ, HD), BF),
            pltpu.VMEM((SEQ, HD), F32),
            pltpu.VMEM((SEQ, HD), F32),
        ],
        compiler_params=params(60),
        cost_estimate=cost(5 * 2 * GROUP * SEQ * SEQ * HD, 6 * MIB, GROUP * SEQ * SEQ),
        name="attend",
    )(queries, grad_attn, rows, col_scale, cos, sin)


def rank_kernel(place, grads, ups, out):
    total = jnp.zeros((PAIR, RANK), F32)
    for r in range(4):
        slot = lax.rem(place[0] + r, 4)
        total += lax.dot_general(grads[slot, :, HD:], ups[r], NT, preferred_element_type=F32)
    out[...] = total


def rank_part(place, grads, ups):
    return pl.pallas_call(
        rank_kernel,
        in_specs=[smem(), whole((4, PAIR, 2 * HD)), whole((4, RANK, HD))],
        out_specs=whole((PAIR, RANK)),
        out_shape=jax.ShapeDtypeStruct((PAIR, RANK), F32),
        compiler_params=params(60),
        cost_estimate=cost(2 * PAIR * 512 * RANK, MIB),
        name="rank_part",
    )(place, grads, ups)


def back_kernel(
    place, grads, own_key, own_val, far, one, two_a, two_b, three, _, mine, theirs,
    left, weights, part, far_sems, line_sems, out_sem,
):
    chunks = near_copies(0, 0, own_key, own_val, far, weights, far_sems)
    chunks += line_copies(NEAR, NEAR, own_key, own_val, one, two_a, two_b, three, weights, line_sems)
    for chunk in chunks:
        start_all(chunk)
    first = pl.multiple_of(place[1] * 128, 128)
    second = pl.multiple_of(128 - place[1] * 128, 128)
    for r in range(4):
        slot = lax.rem(place[0] + r, 4)
        left[:128, r * 256 : (r + 1) * 256] = grads[slot, pl.ds(first, 128), :]
        left[128:, r * 256 : (r + 1) * 256] = grads[slot, pl.ds(second, 128), :]
    leaving = []
    base = 0
    for i, chunk in enumerate(chunks):
        size = CHUNK if i < NEAR // CHUNK else LINE // 2
        wait_all(chunk)
        here = slice(base, base + size)
        part[:, here] = lax.dot_general(left[...], weights[here, :], NT, preferred_element_type=F32).astype(BF)
        cols = pl.ds(base, size)
        leaving += start_all(
            [
                pltpu.make_async_copy(part.at[pl.ds(128, 128), cols], theirs.at[:, cols], out_sem.at[0, i]),
                pltpu.make_async_copy(part.at[pl.ds(0, 128), cols], mine.at[:, cols], out_sem.at[1, i]),
            ]
        )
        base += size
    wait_all(leaving)


def back(place, grads, w_key, w_val, far, line, after):
    count = NEAR // CHUNK
    return pl.pallas_call(
        back_kernel,
        in_specs=[smem(), whole((4, PAIR, 2 * HD))] + [any_ref()] * 8,
        out_specs=[any_ref()] * 2,
        out_shape=[jax.ShapeDtypeStruct((128, D), BF)] * 2,
        scratch_shapes=[
            pltpu.VMEM((PAIR, 1024), BF),
            pltpu.VMEM((D, 1024), BF),
            pltpu.VMEM((PAIR, D), BF),
            pltpu.SemaphoreType.DMA((3, count)),
            pltpu.SemaphoreType.DMA((5, 2)),
            pltpu.SemaphoreType.DMA((2, count + 2)),
        ],
        compiler_params=params(60),
        cost_estimate=cost(2 * PAIR * D * 1024, 20 * MIB),
        name="back",
    )(place, grads, w_key, w_val, far, *line, after)


def join_kernel(place, rank, factor, mine, theirs, out, one, two, result, sems, out_sem):
    size = D // 8
    chunks = []
    for i in range(8):
        cols = pl.ds(i * size, size)
        chunks.append(
            start_all(
                [
                    pltpu.make_async_copy(mine.at[:, cols], one.at[:, cols], sems.at[0, i]),
                    pltpu.make_async_copy(theirs.at[:, cols], two.at[:, cols], sems.at[1, i]),
                ]
            )
        )
    own = rank[pl.ds(pl.multiple_of(place[1] * 128, 128), 128), :]
    leaving = []
    for i, chunk in enumerate(chunks):
        here = slice(i * size, (i + 1) * size)
        adapter = SCALE * jnp.dot(own, factor[:, here], preferred_element_type=F32)
        wait_all(chunk)
        result[:, here] = (one[:, here].astype(F32) + two[:, here].astype(F32) + adapter).astype(BF)
        cols = pl.ds(i * size, size)
        leaving += start_all([pltpu.make_async_copy(result.at[:, cols], out.at[:, cols], out_sem.at[i])])
    wait_all(leaving)


def join(place, rank, factor, mine, theirs):
    return pl.pallas_call(
        join_kernel,
        in_specs=[smem(), whole((PAIR, RANK)), whole((RANK, D)), any_ref(), any_ref()],
        out_specs=any_ref(),
        out_shape=jax.ShapeDtypeStruct((128, D), BF),
        scratch_shapes=[pltpu.VMEM((128, D), BF)] * 3
        + [pltpu.SemaphoreType.DMA((2, 8)), pltpu.SemaphoreType.DMA((8,))],
        compiler_params=params(60),
        cost_estimate=cost(0, 0),
        name="join",
    )(place, rank, factor, mine, theirs)


def down_kernel(place, rank, hid, out):
    part = SCALE * lax.dot_general(rank[...], hid[...], TN, preferred_element_type=F32)
    lane = lax.broadcasted_iota(jnp.int32, (8, HD), 1) // 32
    core = place[1]
    for tile in range(part.shape[1] // HD):
        regs = [part[8 * i : 8 * i + 8, tile * HD : (tile + 1) * HD] for i in range(4)]
        blocks = []
        for pick in range(2):
            column = 2 * pick + core
            block = jnp.zeros((8, HD), F32)
            for i in range(4):
                moved = pltpu.roll(regs[i], lax.rem((i - column + 4) * 32, HD), 1)
                block = jnp.where(lane == i, moved, block)
            blocks.append(block)
        out[16 * tile : 16 * tile + 16, :] = jnp.concatenate(blocks, axis=0).astype(BF)


def down_part(place, rank, pair):
    wide = 2048
    return pl.pallas_call(
        down_kernel,
        grid=(D // wide,),
        in_specs=[smem(), whole((PAIR, RANK)), pl.BlockSpec((PAIR, wide), lambda k: (0, k))],
        out_specs=pl.BlockSpec((wide // 8, HD), lambda k: (k, 0)),
        out_shape=jax.ShapeDtypeStruct((1024, HD), BF),
        compiler_params=params(60),
        cost_estimate=cost(2 * PAIR * D * RANK, 5 * MIB),
        name="down_part",
    )(place, rank, pair)


def finish_kernel(pieces, small, _, out, up_grad, mag_grad):
    total = jnp.sum(pieces[...].astype(F32).reshape(128, 8, HD), axis=0)
    for i in range(4):
        out[8 * i : 8 * i + 8, :] = total[:, 32 * i : 32 * i + 32]
    sums = jnp.sum(small[...], axis=0)
    up_grad[...] = sums[:RANK]
    mag_grad[...] = sums[RANK:]


def finish(pieces, small, after):
    return pl.pallas_call(
        finish_kernel,
        grid=(1,),
        in_specs=[whole((1024, HD)), whole((16, 40, HD)), any_ref()],
        out_specs=[whole((RANK, 32)), whole((RANK, HD)), whole((8, HD))],
        out_shape=[
            jax.ShapeDtypeStruct((RANK, 32), F32),
            jax.ShapeDtypeStruct((RANK, HD), F32),
            jax.ShapeDtypeStruct((8, HD), F32),
        ],
        compiler_params=params(60),
        cost_estimate=cost(0, 0),
        name="finish",
    )(pieces, small, after)


def along_z(value, shift):
    return lax.ppermute(value, ("zh", "zl"), [(i, (i + shift) % 8) for i in range(8)])


def gather_weights(w_key, w_val, up):
    count = NEAR // 16
    at = (lax.axis_index("x") * 4 + lax.axis_index("y")) * count
    seed = jnp.concatenate([lax.dynamic_slice(w, (at, 0), (count, HD)) for w in (w_key, w_val)], axis=1)
    half = count // 2
    first = along_z(seed, -1)
    third = along_z(seed, 1)
    second = jnp.concatenate([along_z(seed[:half], -2), along_z(seed[half:], 2)], axis=0)
    far = lax.all_gather(jnp.concatenate([first, second, third], axis=1), ("x", "y"), axis=0, tiled=True)
    own = jnp.concatenate([w_key[NEAR:], w_val[NEAR:]], axis=1)
    own = jnp.concatenate([jnp.pad(up, ((0, 0), (0, HD))), own], axis=0) + seed[:1, :1] * 0
    one = along_z(own, -1)
    three = along_z(own, 1)
    two_a = along_z(one[: RANK + LINE // 2], -1)
    two_b = along_z(three[RANK + LINE // 2 :], 1)
    ups = jnp.stack([up] + [got[:RANK, :HD] for got in (one, two_a, three)])
    return far, (one, two_a, two_b, three), ups


def shards(hidden, w_key, w_val, factor, up, mag, queries, grad_attn):
    zl, core = lax.axis_index("zl"), lax.axis_index("core")
    place = jnp.stack([zl, core]).astype(jnp.int32)
    swap = [(0, 1), (1, 0)]
    other = lax.ppermute(hidden, "core", swap)
    pair = jnp.where(
        core == 0, jnp.concatenate([hidden, other], axis=0), jnp.concatenate([other, hidden], axis=0)
    )
    down = lax.dot_general(pair, factor, NT, preferred_element_type=F32).astype(BF)
    far, line, ups = gather_weights(w_key, w_val, up)
    merged = w_val.astype(F32) + SCALE * lax.dot_general(factor, up, TN, preferred_element_type=F32)
    norms = jnp.sqrt(jnp.sum(merged * merged, axis=0))
    col_scale = (mag / norms).reshape(1, HD)
    cos, sin = rope_tables()
    cos_here = lax.dynamic_slice(cos, (zl * PAIR, 0), (PAIR, HD))
    sin_here = lax.dynamic_slice(sin, (zl * PAIR, 0), (PAIR, HD))
    so_far = project_line(pair, w_key, w_val, line)
    rows = project(place, pair, w_key, w_val, far, so_far, down, ups, cos_here, sin_here)
    rows = lax.all_to_all(rows, "zl", 0, 0, tiled=True)
    grads, up_grad, mag_grad = attend(queries, grad_attn, rows, col_scale, cos, sin)
    grads = lax.all_to_all(grads.reshape(4, PAIR, 2 * HD), "zl", 0, 0, tiled=True)
    small = jnp.concatenate([up_grad, mag_grad / norms], axis=0)
    small = small + lax.ppermute(small, "zh", swap)
    padded = jnp.pad(small, ((0, 88), (0, 0)))
    small = lax.all_gather(padded, ("x", "y"), axis=0, tiled=True)
    part = rank_part(place, grads, ups)
    rank = (part + lax.ppermute(part, "core", swap)).astype(BF)
    mine, theirs = back(place, grads, w_key, w_val, far, line, padded)
    theirs = lax.ppermute(theirs, "core", swap)
    pieces = lax.all_to_all(down_part(place, rank, pair), DP + ("zl",), 0, 0, tiled=True)
    grad_hidden = join(place, rank, factor, mine, theirs)
    grad_down, up_sum, mag_sum = finish(pieces, small.reshape(16, HD, HD), grad_hidden)
    return grad_hidden, grad_down, up_sum, mag_sum[0]


def solution(mesh):
    fine = Mesh(np.asarray(mesh.devices).reshape(4, 4, 2, 4, 2), EVERY)
    tensor = ("zl", "core")
    return jax.shard_map(
        shards,
        mesh=fine,
        in_specs=(
            P(EVERY, None),
            P(None, tensor),
            P(None, tensor),
            P(),
            P(None, tensor),
            P(tensor),
            P(DP, tensor),
            P(DP, tensor),
        ),
        out_specs=(P(EVERY, None), P(None, EVERY), P(None, tensor), P(tensor)),
        check_vma=False,
    )
```

```python
import jax
import jax.numpy as jnp
import numpy as np
from jax import lax
from jax.experimental import pallas as pl
from jax.experimental.pallas import tpu as pltpu
from jax.sharding import Mesh, PartitionSpec as P

HD = 128
D = 8192
SEQ = 1024
RANK = 32
PAIR = 256
NEAR = 5120
LINE = 3072
CHUNK = 1280
QB = 256
GROUP = 4
HEADS = 2
SMALL = 256
SCALE = 2.0
ROPE_BASE = 500000.0
LOG2E = 1.4426950408889634
INV_SQRT = HD ** (-0.5)
MIB = 1024 * 1024
BF = jnp.bfloat16
F32 = jnp.float32
NT = (((1,), (1,)), ((), ()))
TN = (((0,), (0,)), ((), ()))
EVERY = ("x", "y", "zh", "zl", "core")
DP = ("x", "y", "zh")


def rope_tables():
    half = HD // 2
    frequency = ROPE_BASE ** (-(jnp.arange(half, dtype=F32) * 2.0 / HD))
    angles = jnp.arange(SEQ, dtype=F32)[:, None] * frequency[None, :]
    cosine, sine = jnp.cos(angles), jnp.sin(angles)
    return jnp.concatenate([cosine, cosine], 1), jnp.concatenate([-sine, sine], 1)


def smem():
    return pl.BlockSpec(memory_space=pltpu.SMEM)


def whole(shape):
    return pl.BlockSpec(shape, lambda *_: (0,) * len(shape))


def params(limit):
    return pltpu.CompilerParams(vmem_limit_bytes=limit * MIB)


def cost(flops, moved, trans=0):
    return pl.CostEstimate(flops=flops, bytes_accessed=moved, transcendentals=trans)


def any_ref():
    return pl.BlockSpec(memory_space=pl.ANY)


def start_all(copies):
    for copy in copies:
        copy.start()
    return copies


def wait_all(copies):
    for copy in copies:
        copy.wait()


def near_copies(base, first, own_key, own_val, far, weights, sems):
    chunks = []
    for i in range(far.shape[0] // CHUNK):
        here = pl.ds(first + i * CHUNK, CHUNK)
        near = pl.ds(i * CHUNK, CHUNK)
        there = pl.ds(base + i * CHUNK, CHUNK)
        chunks.append(
            [
                pltpu.make_async_copy(own_key.at[there, :], weights.at[here, pl.ds(0, HD)], sems.at[0, i]),
                pltpu.make_async_copy(own_val.at[there, :], weights.at[here, pl.ds(HD, HD)], sems.at[1, i]),
                pltpu.make_async_copy(far.at[near, :], weights.at[here, pl.ds(256, 768)], sems.at[2, i]),
            ]
        )
    return chunks


def line_copies(base, first, own_key, own_val, one, two_a, two_b, three, weights, sems):
    chunks = []
    size = LINE // 2
    for i, two in enumerate((two_a.at[pl.ds(RANK, size), :], two_b)):
        here = pl.ds(first + i * size, size)
        there = pl.ds(base + i * size, size)
        near = pl.ds(RANK + i * size, size)
        chunks.append(
            [
                pltpu.make_async_copy(own_key.at[there, :], weights.at[here, pl.ds(0, HD)], sems.at[0, i]),
                pltpu.make_async_copy(own_val.at[there, :], weights.at[here, pl.ds(HD, HD)], sems.at[1, i]),
                pltpu.make_async_copy(one.at[near, :], weights.at[here, pl.ds(256, 256)], sems.at[2, i]),
                pltpu.make_async_copy(two, weights.at[here, pl.ds(512, 256)], sems.at[3, i]),
                pltpu.make_async_copy(three.at[near, :], weights.at[here, pl.ds(768, 256)], sems.at[4, i]),
            ]
        )
    return chunks


def pair_copies(pair, hid, base, count, sem):
    size = hid.shape[1] // count
    return [
        pltpu.make_async_copy(
            pair.at[:, pl.ds(base + i * size, size)], hid.at[:, pl.ds(i * size, size)], sem.at[i]
        )
        for i in range(count)
    ]


def multiply(acc, chunks, hid_chunks, hid, weights):
    size = hid.shape[1] // len(chunks)
    for i, chunk in enumerate(chunks):
        wait_all(chunk + [hid_chunks[i]])
        here = slice(i * size, (i + 1) * size)
        term = jnp.dot(hid[:, here], weights[here, :], preferred_element_type=F32)
        acc = term if acc is None else acc + term
    return acc


def project_line_kernel(
    pair, own_key, own_val, one, two_a, two_b, three, out, hid, weights, hid_sem, sems
):
    chunks = line_copies(NEAR, 0, own_key, own_val, one, two_a, two_b, three, weights, sems)
    hid_chunks = pair_copies(pair, hid, NEAR, 2, hid_sem)
    for i in range(2):
        start_all(chunks[i] + [hid_chunks[i]])
    out[...] = multiply(None, chunks, hid_chunks, hid, weights)


def project_line(pair, w_key, w_val, line):
    return pl.pallas_call(
        project_line_kernel,
        in_specs=[any_ref()] * 7,
        out_specs=whole((PAIR, 1024)),
        out_shape=jax.ShapeDtypeStruct((PAIR, 1024), F32),
        scratch_shapes=[
            pltpu.VMEM((PAIR, LINE), BF),
            pltpu.VMEM((LINE, 1024), BF),
            pltpu.SemaphoreType.DMA((2,)),
            pltpu.SemaphoreType.DMA((5, 2)),
        ],
        compiler_params=params(60),
        cost_estimate=cost(2 * PAIR * LINE * 1024, 8 * MIB),
        name="project_line",
    )(pair, w_key, w_val, *line)


def project_kernel(
    place, pair, own_key, own_val, far, so_far, down, ups, cos, sin, out, hid, weights, hid_sem, sems
):
    count = NEAR // CHUNK
    chunks = near_copies(0, 0, own_key, own_val, far, weights, sems)
    hid_chunks = pair_copies(pair, hid, 0, count, hid_sem)
    for i in range(count):
        start_all(chunks[i] + [hid_chunks[i]])
    acc = multiply(so_far[...], chunks, hid_chunks, hid, weights)
    packed = jnp.concatenate([down[64 * j : 64 * j + 64, :] for j in range(4)], axis=1)
    packed = jnp.concatenate([packed[:32], packed[32:], jnp.zeros((32, HD), BF)], axis=1)
    for r in range(4):
        key = acc[:, r * 256 : r * 256 + HD]
        turned = key * cos[...] + pltpu.roll(key, HD // 2, 1) * sin[...]
        turned = turned * (INV_SQRT * LOG2E)
        high = turned.astype(BF)
        low = (turned - high.astype(F32)).astype(BF)
        lifted = jnp.dot(down[...], ups[r], preferred_element_type=F32)
        base = (acc[:, r * 256 + HD : (r + 1) * 256] + SCALE * lifted).astype(BF)
        slot = lax.rem(place[0] + r, 4)
        out[slot, :PAIR, :] = jnp.concatenate([high, low, base], axis=1)
        out[slot, PAIR:, :] = packed


def project(place, pair, w_key, w_val, far, so_far, down, ups, cos, sin):
    count = NEAR // CHUNK
    return pl.pallas_call(
        project_kernel,
        in_specs=[
            smem(),
            any_ref(),
            any_ref(),
            any_ref(),
            any_ref(),
            whole((PAIR, 1024)),
            whole((PAIR, RANK)),
            whole((4, RANK, HD)),
            whole((PAIR, HD)),
            whole((PAIR, HD)),
        ],
        out_specs=whole((4, PAIR + 32, 3 * HD)),
        out_shape=jax.ShapeDtypeStruct((4, PAIR + 32, 3 * HD), BF),
        scratch_shapes=[
            pltpu.VMEM((PAIR, NEAR), BF),
            pltpu.VMEM((NEAR, 1024), BF),
            pltpu.SemaphoreType.DMA((count,)),
            pltpu.SemaphoreType.DMA((3, count)),
        ],
        compiler_params=params(60),
        cost_estimate=cost(2 * PAIR * NEAR * 1024, 14 * MIB),
        name="project",
    )(place, pair, w_key, w_val, far, so_far, down, ups, cos, sin)


def attend_kernel(query, grad, rows, col_scale, norms, cos, sin, grads, small, keys, vals, dkey, dval):
    step = pl.program_id(0)

    @pl.when(step == 0)
    def _():
        for i in range(4):
            here = slice(i * PAIR, (i + 1) * PAIR)
            keys[here, :] = rows[i, :PAIR, : 2 * HD]
            vals[here, :] = (rows[i, :PAIR, 2 * HD :].astype(F32) * col_scale[...]).astype(BF)
        dkey[...] = jnp.zeros_like(dkey)
        dval[...] = jnp.zeros_like(dval)

    for block in range(SEQ // QB):
        stop = (block + 1) * QB
        here = slice(block * QB, stop)
        queries, outs, halves, sgrads = [], [], [], []
        for head in range(HEADS):
            q = query[here, head * HD : (head + 1) * HD]
            g = grad[here, head * HD : (head + 1) * HD]
            qq = jnp.concatenate([q, q], axis=1)
            scores = lax.dot_general(keys[:stop], qq, NT, preferred_element_type=F32)
            key_at = lax.broadcasted_iota(jnp.int32, (QB, QB), 0)
            query_at = lax.broadcasted_iota(jnp.int32, (QB, QB), 1)
            edge = jnp.where(key_at <= query_at, scores[block * QB :], -1e30)
            if block:
                scores = jnp.concatenate([scores[: block * QB], edge], axis=0)
            else:
                scores = edge
            powers = jnp.exp2(scores - jnp.max(scores, axis=0, keepdims=True))
            attn = powers * (1.0 / jnp.sum(powers, axis=0, keepdims=True))
            half = attn.astype(BF)
            pgrad = lax.dot_general(vals[:stop], g, NT, preferred_element_type=F32)
            delta = jnp.sum(half.astype(F32) * pgrad, axis=0, keepdims=True)
            sgrads.append((attn * (pgrad - delta)).astype(BF))
            halves.append(half)
            queries.append(q)
            outs.append(g)
        dval[:stop] += jnp.dot(
            jnp.concatenate(halves, 1), jnp.concatenate(outs, 0), preferred_element_type=F32
        )
        dkey[:stop] += jnp.dot(
            jnp.concatenate(sgrads, 1), jnp.concatenate(queries, 0), preferred_element_type=F32
        )

    @pl.when(step == pl.num_programs(0) - 1)
    def _():
        dk = dkey[...] * INV_SQRT
        dk = dk * cos[...] - pltpu.roll(dk, HD // 2, 1) * sin[...]
        dv = dval[...]
        gv = (dv * col_scale[...]).astype(BF)
        grads[:, :HD] = dk.astype(BF)
        grads[:, HD:] = gv
        total = jnp.zeros((RANK, HD), F32)
        mags = jnp.zeros((1, HD), F32)
        for i in range(4):
            here = slice(i * PAIR, (i + 1) * PAIR)
            packed = rows[i, PAIR:, : 2 * HD]
            packed = jnp.concatenate([packed[:, :HD], packed[:, HD:]], axis=0)
            down = jnp.concatenate([packed[:, 32 * j : 32 * j + 32] for j in range(4)], axis=0)
            total += lax.dot_general(down, gv[here], TN, preferred_element_type=F32)
            mags += jnp.sum(dv[here] * rows[i, :PAIR, 2 * HD :].astype(F32), axis=0, keepdims=True)
        small[:RANK, :] = SCALE * total
        small[RANK:, :] = jnp.broadcast_to(mags / norms[...], (SMALL - RANK, HD))


def attend(queries, grad_attn, rows, col_scale, norms, cos, sin):
    return pl.pallas_call(
        attend_kernel,
        grid=(GROUP // HEADS,),
        in_specs=[
            pl.BlockSpec((SEQ, HEADS * HD), lambda h: (0, h)),
            pl.BlockSpec((SEQ, HEADS * HD), lambda h: (0, h)),
            whole((4, PAIR + 32, 3 * HD)),
            whole((1, HD)),
            whole((1, HD)),
            whole((SEQ, HD)),
            whole((SEQ, HD)),
        ],
        out_specs=[whole((SEQ, 2 * HD)), whole((SMALL, HD))],
        out_shape=[jax.ShapeDtypeStruct((SEQ, 2 * HD), BF), jax.ShapeDtypeStruct((SMALL, HD), F32)],
        scratch_shapes=[
            pltpu.VMEM((SEQ, 2 * HD), BF),
            pltpu.VMEM((SEQ, HD), BF),
            pltpu.VMEM((SEQ, HD), F32),
            pltpu.VMEM((SEQ, HD), F32),
        ],
        compiler_params=params(60),
        cost_estimate=cost(5 * 2 * GROUP * SEQ * SEQ * HD, 6 * MIB, GROUP * SEQ * SEQ),
        name="attend",
    )(queries, grad_attn, rows, col_scale, norms, cos, sin)


def rank_kernel(place, grads, ups, out):
    total = jnp.zeros((PAIR, RANK), F32)
    for r in range(4):
        slot = lax.rem(place[0] + r, 4)
        total += lax.dot_general(grads[slot, :, HD:], ups[r], NT, preferred_element_type=F32)
    out[...] = total


def rank_part(place, grads, ups):
    return pl.pallas_call(
        rank_kernel,
        in_specs=[smem(), whole((4, PAIR, 2 * HD)), whole((4, RANK, HD))],
        out_specs=whole((PAIR, RANK)),
        out_shape=jax.ShapeDtypeStruct((PAIR, RANK), F32),
        compiler_params=params(60),
        cost_estimate=cost(2 * PAIR * 512 * RANK, MIB),
        name="rank_part",
    )(place, grads, ups)


def back_kernel(
    place, grads, own_key, own_val, far, one, two_a, two_b, three, _, mine, theirs,
    left, weights, part, far_sems, line_sems, out_sem,
):
    chunks = near_copies(0, 0, own_key, own_val, far, weights, far_sems)
    chunks += line_copies(NEAR, NEAR, own_key, own_val, one, two_a, two_b, three, weights, line_sems)
    for chunk in chunks:
        start_all(chunk)
    first = pl.multiple_of(place[1] * 128, 128)
    second = pl.multiple_of(128 - place[1] * 128, 128)
    for r in range(4):
        slot = lax.rem(place[0] + r, 4)
        left[:128, r * 256 : (r + 1) * 256] = grads[slot, pl.ds(first, 128), :]
        left[128:, r * 256 : (r + 1) * 256] = grads[slot, pl.ds(second, 128), :]
    leaving = []
    base = 0
    for i, chunk in enumerate(chunks):
        size = CHUNK if i < NEAR // CHUNK else LINE // 2
        wait_all(chunk)
        here = slice(base, base + size)
        part[:, here] = lax.dot_general(left[...], weights[here, :], NT, preferred_element_type=F32).astype(BF)
        cols = pl.ds(base, size)
        leaving += start_all(
            [
                pltpu.make_async_copy(part.at[pl.ds(128, 128), cols], theirs.at[:, cols], out_sem.at[0, i]),
                pltpu.make_async_copy(part.at[pl.ds(0, 128), cols], mine.at[:, cols], out_sem.at[1, i]),
            ]
        )
        base += size
    wait_all(leaving)


def back(place, grads, w_key, w_val, far, line, after):
    count = NEAR // CHUNK
    return pl.pallas_call(
        back_kernel,
        in_specs=[smem(), whole((4, PAIR, 2 * HD))] + [any_ref()] * 8,
        out_specs=[any_ref()] * 2,
        out_shape=[jax.ShapeDtypeStruct((128, D), BF)] * 2,
        scratch_shapes=[
            pltpu.VMEM((PAIR, 1024), BF),
            pltpu.VMEM((D, 1024), BF),
            pltpu.VMEM((PAIR, D), BF),
            pltpu.SemaphoreType.DMA((3, count)),
            pltpu.SemaphoreType.DMA((5, 2)),
            pltpu.SemaphoreType.DMA((2, count + 2)),
        ],
        compiler_params=params(60),
        cost_estimate=cost(0, 0),
        name="back",
    )(place, grads, w_key, w_val, far, *line, after)


def join_kernel(place, rank, factor, mine, theirs, _, out, one, two, result, sems, out_sem):
    size = D // 8
    chunks = []
    for i in range(8):
        cols = pl.ds(i * size, size)
        chunks.append(
            start_all(
                [
                    pltpu.make_async_copy(mine.at[:, cols], one.at[:, cols], sems.at[0, i]),
                    pltpu.make_async_copy(theirs.at[:, cols], two.at[:, cols], sems.at[1, i]),
                ]
            )
        )
    own = rank[pl.ds(pl.multiple_of(place[1] * 128, 128), 128), :]
    leaving = []
    for i, chunk in enumerate(chunks):
        here = slice(i * size, (i + 1) * size)
        adapter = SCALE * jnp.dot(own, factor[:, here], preferred_element_type=F32)
        wait_all(chunk)
        result[:, here] = (one[:, here].astype(F32) + two[:, here].astype(F32) + adapter).astype(BF)
        cols = pl.ds(i * size, size)
        leaving += start_all([pltpu.make_async_copy(result.at[:, cols], out.at[:, cols], out_sem.at[i])])
    wait_all(leaving)


def join(place, rank, factor, mine, theirs, after):
    return pl.pallas_call(
        join_kernel,
        in_specs=[smem(), whole((PAIR, RANK)), whole((RANK, D))] + [any_ref()] * 3,
        out_specs=any_ref(),
        out_shape=jax.ShapeDtypeStruct((128, D), BF),
        scratch_shapes=[pltpu.VMEM((128, D), BF)] * 3
        + [pltpu.SemaphoreType.DMA((2, 8)), pltpu.SemaphoreType.DMA((8,))],
        compiler_params=params(60),
        cost_estimate=cost(0, 0),
        name="join",
    )(place, rank, factor, mine, theirs, after)


def down_kernel(place, part, got, hid, out, rank):
    rank[...] = (part[...] + got[...]).astype(BF)
    product = SCALE * lax.dot_general(rank[...], hid[...], TN, preferred_element_type=F32)
    lane = lax.broadcasted_iota(jnp.int32, (8, HD), 1) // 32
    core = place[1]
    for tile in range(product.shape[1] // HD):
        regs = [product[8 * i : 8 * i + 8, tile * HD : (tile + 1) * HD] for i in range(4)]
        blocks = []
        for pick in range(2):
            column = 2 * pick + core
            block = jnp.zeros((8, HD), F32)
            for i in range(4):
                moved = pltpu.roll(regs[i], lax.rem((i - column + 4) * 32, HD), 1)
                block = jnp.where(lane == i, moved, block)
            blocks.append(block)
        out[16 * tile : 16 * tile + 16, :] = jnp.concatenate(blocks, axis=0).astype(BF)


def down_part(place, part, got, pair):
    wide = 2048
    return pl.pallas_call(
        down_kernel,
        grid=(D // wide,),
        in_specs=[
            smem(),
            whole((PAIR, RANK)),
            whole((PAIR, RANK)),
            pl.BlockSpec((PAIR, wide), lambda k: (0, k)),
        ],
        out_specs=[pl.BlockSpec((wide // 8, HD), lambda k: (k, 0)), whole((PAIR, RANK))],
        out_shape=[jax.ShapeDtypeStruct((1024, HD), BF), jax.ShapeDtypeStruct((PAIR, RANK), BF)],
        compiler_params=params(60),
        cost_estimate=cost(2 * PAIR * D * RANK, 5 * MIB),
        name="down_part",
    )(place, part, got, pair)


def fold_kernel(small, out):
    out[...] = jnp.sum(small[...], axis=0)


def fold(small):
    return pl.pallas_call(
        fold_kernel,
        grid=(1,),
        in_specs=[whole((16, 40, HD))],
        out_specs=whole((40, HD)),
        out_shape=jax.ShapeDtypeStruct((40, HD), F32),
        compiler_params=params(60),
        cost_estimate=cost(0, 0),
        name="fold",
    )(small)


def finish_kernel(pieces, small, other, _, out, up_grad, mag_grad):
    total = jnp.sum(pieces[...].astype(F32).reshape(128, 8, HD), axis=0)
    for i in range(4):
        out[8 * i : 8 * i + 8, :] = total[:, 32 * i : 32 * i + 32]
    sums = small[...] + other[...]
    up_grad[...] = sums[:RANK]
    mag_grad[...] = sums[RANK:]


def finish(pieces, small, other, after):
    return pl.pallas_call(
        finish_kernel,
        in_specs=[whole((1024, HD)), whole((40, HD)), whole((40, HD)), any_ref()],
        out_specs=[whole((RANK, 32)), whole((RANK, HD)), whole((8, HD))],
        out_shape=[
            jax.ShapeDtypeStruct((RANK, 32), F32),
            jax.ShapeDtypeStruct((RANK, HD), F32),
            jax.ShapeDtypeStruct((8, HD), F32),
        ],
        compiler_params=params(60),
        cost_estimate=cost(0, 0),
        name="finish",
    )(pieces, small, other, after)


def along_z(value, shift):
    return lax.ppermute(value, ("zh", "zl"), [(i, (i + shift) % 8) for i in range(8)])


def gather_weights(w_key, w_val, up):
    count = NEAR // 16
    at = (lax.axis_index("x") * 4 + lax.axis_index("y")) * count
    seed = jnp.concatenate([lax.dynamic_slice(w, (at, 0), (count, HD)) for w in (w_key, w_val)], axis=1)
    half = count // 2
    first = along_z(seed, -1)
    third = along_z(seed, 1)
    second = jnp.concatenate([along_z(seed[:half], -2), along_z(seed[half:], 2)], axis=0)
    far = lax.all_gather(jnp.concatenate([first, second, third], axis=1), ("x", "y"), axis=0, tiled=True)
    own = jnp.concatenate([w_key[NEAR:], w_val[NEAR:]], axis=1)
    own = jnp.concatenate([jnp.pad(up, ((0, 0), (0, HD))), own], axis=0) + seed[:1, :1] * 0
    one = along_z(own, -1)
    three = along_z(own, 1)
    two_a = along_z(one[: RANK + LINE // 2], -1)
    two_b = along_z(three[RANK + LINE // 2 :], 1)
    ups = jnp.stack([up] + [got[:RANK, :HD] for got in (one, two_a, three)])
    return far, (one, two_a, two_b, three), ups


def shards(hidden, w_key, w_val, factor, up, mag, queries, grad_attn):
    zl, core = lax.axis_index("zl"), lax.axis_index("core")
    place = jnp.stack([zl, core]).astype(jnp.int32)
    swap = [(0, 1), (1, 0)]
    other = lax.ppermute(hidden, "core", swap)
    pair = jnp.where(
        core == 0, jnp.concatenate([hidden, other], axis=0), jnp.concatenate([other, hidden], axis=0)
    )
    down = lax.dot_general(pair, factor, NT, preferred_element_type=F32).astype(BF)
    far, line, ups = gather_weights(w_key, w_val, up)
    merged = w_val.astype(F32) + SCALE * lax.dot_general(factor, up, TN, preferred_element_type=F32)
    norms = jnp.sqrt(jnp.sum(merged * merged, axis=0))
    col_scale = (mag / norms).reshape(1, HD)
    cos, sin = rope_tables()
    cos_here = lax.dynamic_slice(cos, (zl * PAIR, 0), (PAIR, HD))
    sin_here = lax.dynamic_slice(sin, (zl * PAIR, 0), (PAIR, HD))
    so_far = project_line(pair, w_key, w_val, line)
    rows = project(place, pair, w_key, w_val, far, so_far, down, ups, cos_here, sin_here)
    rows = lax.all_to_all(rows, "zl", 0, 0, tiled=True)
    grads, small = attend(queries, grad_attn, rows, col_scale, norms.reshape(1, HD), cos, sin)
    grads = lax.all_to_all(grads.reshape(4, PAIR, 2 * HD), "zl", 0, 0, tiled=True)
    gathered = lax.all_gather(small, ("x", "y"), axis=0, tiled=True)
    part = rank_part(place, grads, ups)
    got = lax.ppermute(part, "core", swap)
    mine, theirs = back(place, grads, w_key, w_val, far, line, small)
    theirs = lax.ppermute(theirs, "core", swap)
    pieces, rank = down_part(place, part, got, pair)
    pieces = lax.all_to_all(pieces, DP + ("zl",), 0, 0, tiled=True)
    small = fold(gathered.reshape(16, SMALL, HD))
    other = lax.ppermute(small, "zh", swap)
    grad_hidden = join(place, rank, factor, mine, theirs, small)
    grad_down, up_sum, mag_sum = finish(pieces, small, other, grad_hidden)
    return grad_hidden, grad_down, up_sum, mag_sum[0]


def solution(mesh):
    fine = Mesh(np.asarray(mesh.devices).reshape(4, 4, 2, 4, 2), EVERY)
    tensor = ("zl", "core")
    return jax.shard_map(
        shards,
        mesh=fine,
        in_specs=(
            P(EVERY, None),
            P(None, tensor),
            P(None, tensor),
            P(),
            P(None, tensor),
            P(tensor),
            P(DP, tensor),
            P(DP, tensor),
        ),
        out_specs=(P(EVERY, None), P(None, EVERY), P(None, tensor), P(tensor)),
        check_vma=False,
    )
```

```python
import jax
import jax.numpy as jnp
import numpy as np
from jax import lax
from jax.experimental import pallas as pl
from jax.experimental.pallas import tpu as pltpu
from jax.sharding import Mesh, PartitionSpec as P

HD = 128
D = 8192
SEQ = 1024
RANK = 32
PAIR = 256
NEAR = 5120
LINE = 3072
CHUNK = 1280
QB = 256
GROUP = 4
HEADS = 2
SMALL = 256
SCALE = 2.0
ROPE_BASE = 500000.0
LOG2E = 1.4426950408889634
INV_SQRT = HD ** (-0.5)
MIB = 1024 * 1024
BF = jnp.bfloat16
F32 = jnp.float32
NT = (((1,), (1,)), ((), ()))
TN = (((0,), (0,)), ((), ()))
EVERY = ("x", "y", "zh", "zl", "core")
DP = ("x", "y", "zh")


def rope_tables():
    half = HD // 2
    frequency = ROPE_BASE ** (-(jnp.arange(half, dtype=F32) * 2.0 / HD))
    angles = jnp.arange(SEQ, dtype=F32)[:, None] * frequency[None, :]
    cosine, sine = jnp.cos(angles), jnp.sin(angles)
    return jnp.concatenate([cosine, cosine], 1), jnp.concatenate([-sine, sine], 1)


def smem():
    return pl.BlockSpec(memory_space=pltpu.SMEM)


def whole(shape):
    return pl.BlockSpec(shape, lambda *_: (0,) * len(shape))


def params(limit):
    return pltpu.CompilerParams(vmem_limit_bytes=limit * MIB)


def cost(flops, moved, trans=0):
    return pl.CostEstimate(flops=flops, bytes_accessed=moved, transcendentals=trans)


def in_vmem():
    return pl.BlockSpec(memory_space=pltpu.VMEM)


def any_ref():
    return pl.BlockSpec(memory_space=pl.ANY)


def start_all(copies):
    for copy in copies:
        copy.start()
    return copies


def wait_all(copies):
    for copy in copies:
        copy.wait()


def near_copies(base, first, own_key, own_val, far, weights, sems):
    chunks = []
    for i in range(far.shape[0] // CHUNK):
        here = pl.ds(first + i * CHUNK, CHUNK)
        near = pl.ds(i * CHUNK, CHUNK)
        there = pl.ds(base + i * CHUNK, CHUNK)
        chunks.append(
            [
                pltpu.make_async_copy(own_key.at[there, :], weights.at[here, pl.ds(0, HD)], sems.at[0, i]),
                pltpu.make_async_copy(own_val.at[there, :], weights.at[here, pl.ds(HD, HD)], sems.at[1, i]),
                pltpu.make_async_copy(far.at[near, :], weights.at[here, pl.ds(256, 768)], sems.at[2, i]),
            ]
        )
    return chunks


def line_copies(base, first, own_key, own_val, one, two_a, two_b, three, weights, sems):
    chunks = []
    size = LINE // 2
    for i, two in enumerate((two_a.at[pl.ds(RANK, size), :], two_b)):
        here = pl.ds(first + i * size, size)
        there = pl.ds(base + i * size, size)
        near = pl.ds(RANK + i * size, size)
        chunks.append(
            [
                pltpu.make_async_copy(own_key.at[there, :], weights.at[here, pl.ds(0, HD)], sems.at[0, i]),
                pltpu.make_async_copy(own_val.at[there, :], weights.at[here, pl.ds(HD, HD)], sems.at[1, i]),
                pltpu.make_async_copy(one.at[near, :], weights.at[here, pl.ds(256, 256)], sems.at[2, i]),
                pltpu.make_async_copy(two, weights.at[here, pl.ds(512, 256)], sems.at[3, i]),
                pltpu.make_async_copy(three.at[near, :], weights.at[here, pl.ds(768, 256)], sems.at[4, i]),
            ]
        )
    return chunks


def pair_copies(pair, hid, base, count, sem):
    size = hid.shape[1] // count
    return [
        pltpu.make_async_copy(
            pair.at[:, pl.ds(base + i * size, size)], hid.at[:, pl.ds(i * size, size)], sem.at[i]
        )
        for i in range(count)
    ]


def multiply(acc, chunks, hid_chunks, hid, weights):
    size = hid.shape[1] // len(chunks)
    for i, chunk in enumerate(chunks):
        wait_all(chunk + [hid_chunks[i]])
        here = slice(i * size, (i + 1) * size)
        term = jnp.dot(hid[:, here], weights[here, :], preferred_element_type=F32)
        acc = term if acc is None else acc + term
    return acc


def project_line_kernel(
    pair, own_key, own_val, one, two_a, two_b, three, out, hid, weights, hid_sem, sems
):
    chunks = line_copies(NEAR, 0, own_key, own_val, one, two_a, two_b, three, weights, sems)
    hid_chunks = pair_copies(pair, hid, NEAR, 2, hid_sem)
    for i in range(2):
        start_all(chunks[i] + [hid_chunks[i]])
    out[...] = multiply(None, chunks, hid_chunks, hid, weights)


def project_line(pair, w_key, w_val, line):
    return pl.pallas_call(
        project_line_kernel,
        in_specs=[any_ref()] * 7,
        out_specs=whole((PAIR, 1024)),
        out_shape=jax.ShapeDtypeStruct((PAIR, 1024), F32),
        scratch_shapes=[
            pltpu.VMEM((PAIR, LINE), BF),
            pltpu.VMEM((LINE, 1024), BF),
            pltpu.SemaphoreType.DMA((2,)),
            pltpu.SemaphoreType.DMA((5, 2)),
        ],
        compiler_params=params(60),
        cost_estimate=cost(2 * PAIR * LINE * 1024, 8 * MIB),
        name="project_line",
    )(pair, w_key, w_val, *line)


def project_kernel(
    place, pair, own_key, own_val, far, so_far, down, ups, cos, sin, out, hid, weights, hid_sem, sems
):
    count = NEAR // CHUNK
    chunks = near_copies(0, 0, own_key, own_val, far, weights, sems)
    hid_chunks = pair_copies(pair, hid, 0, count, hid_sem)
    for i in range(count):
        start_all(chunks[i] + [hid_chunks[i]])
    acc = multiply(so_far[...], chunks, hid_chunks, hid, weights)
    packed = jnp.concatenate([down[64 * j : 64 * j + 64, :] for j in range(4)], axis=1)
    packed = jnp.concatenate([packed[:32], packed[32:], jnp.zeros((32, HD), BF)], axis=1)
    for r in range(4):
        key = acc[:, r * 256 : r * 256 + HD]
        turned = key * cos[...] + pltpu.roll(key, HD // 2, 1) * sin[...]
        turned = turned * (INV_SQRT * LOG2E)
        high = turned.astype(BF)
        low = (turned - high.astype(F32)).astype(BF)
        lifted = jnp.dot(down[...], ups[r], preferred_element_type=F32)
        base = (acc[:, r * 256 + HD : (r + 1) * 256] + SCALE * lifted).astype(BF)
        slot = lax.rem(place[0] + r, 4)
        out[slot, :PAIR, :] = jnp.concatenate([high, low, base], axis=1)
        out[slot, PAIR:, :] = packed


def project(place, pair, w_key, w_val, far, so_far, down, ups, cos, sin):
    count = NEAR // CHUNK
    return pl.pallas_call(
        project_kernel,
        in_specs=[
            smem(),
            any_ref(),
            any_ref(),
            any_ref(),
            any_ref(),
            whole((PAIR, 1024)),
            whole((PAIR, RANK)),
            whole((4, RANK, HD)),
            whole((PAIR, HD)),
            whole((PAIR, HD)),
        ],
        out_specs=whole((4, PAIR + 32, 3 * HD)),
        out_shape=jax.ShapeDtypeStruct((4, PAIR + 32, 3 * HD), BF),
        scratch_shapes=[
            pltpu.VMEM((PAIR, NEAR), BF),
            pltpu.VMEM((NEAR, 1024), BF),
            pltpu.SemaphoreType.DMA((count,)),
            pltpu.SemaphoreType.DMA((3, count)),
        ],
        compiler_params=params(60),
        cost_estimate=cost(2 * PAIR * NEAR * 1024, 14 * MIB),
        name="project",
    )(place, pair, w_key, w_val, far, so_far, down, ups, cos, sin)


def attend_kernel(query, grad, rows, col_scale, norms, cos, sin, grads, small, keys, vals, dkey, dval):
    step = pl.program_id(0)

    @pl.when(step == 0)
    def _():
        for i in range(4):
            here = slice(i * PAIR, (i + 1) * PAIR)
            keys[here, :] = rows[i, :PAIR, : 2 * HD]
            vals[here, :] = (rows[i, :PAIR, 2 * HD :].astype(F32) * col_scale[...]).astype(BF)
        dkey[...] = jnp.zeros_like(dkey)
        dval[...] = jnp.zeros_like(dval)

    for block in range(SEQ // QB):
        stop = (block + 1) * QB
        here = slice(block * QB, stop)
        queries, outs, halves, sgrads = [], [], [], []
        for head in range(HEADS):
            q = query[here, head * HD : (head + 1) * HD]
            g = grad[here, head * HD : (head + 1) * HD]
            qq = jnp.concatenate([q, q], axis=1)
            scores = lax.dot_general(keys[:stop], qq, NT, preferred_element_type=F32)
            key_at = lax.broadcasted_iota(jnp.int32, (QB, QB), 0)
            query_at = lax.broadcasted_iota(jnp.int32, (QB, QB), 1)
            edge = jnp.where(key_at <= query_at, scores[block * QB :], -1e30)
            if block:
                scores = jnp.concatenate([scores[: block * QB], edge], axis=0)
            else:
                scores = edge
            powers = jnp.exp2(scores - jnp.max(scores, axis=0, keepdims=True))
            attn = powers * (1.0 / jnp.sum(powers, axis=0, keepdims=True))
            half = attn.astype(BF)
            pgrad = lax.dot_general(vals[:stop], g, NT, preferred_element_type=F32)
            delta = jnp.sum(half.astype(F32) * pgrad, axis=0, keepdims=True)
            sgrads.append((attn * (pgrad - delta)).astype(BF))
            halves.append(half)
            queries.append(q)
            outs.append(g)
        dval[:stop] += jnp.dot(
            jnp.concatenate(halves, 1), jnp.concatenate(outs, 0), preferred_element_type=F32
        )
        dkey[:stop] += jnp.dot(
            jnp.concatenate(sgrads, 1), jnp.concatenate(queries, 0), preferred_element_type=F32
        )

    @pl.when(step == pl.num_programs(0) - 1)
    def _():
        dk = dkey[...] * INV_SQRT
        dk = dk * cos[...] - pltpu.roll(dk, HD // 2, 1) * sin[...]
        dv = dval[...]
        gv = (dv * col_scale[...]).astype(BF)
        grads[:, :HD] = dk.astype(BF)
        grads[:, HD:] = gv
        total = jnp.zeros((RANK, HD), F32)
        mags = jnp.zeros((1, HD), F32)
        for i in range(4):
            here = slice(i * PAIR, (i + 1) * PAIR)
            packed = rows[i, PAIR:, : 2 * HD]
            packed = jnp.concatenate([packed[:, :HD], packed[:, HD:]], axis=0)
            down = jnp.concatenate([packed[:, 32 * j : 32 * j + 32] for j in range(4)], axis=0)
            total += lax.dot_general(down, gv[here], TN, preferred_element_type=F32)
            mags += jnp.sum(dv[here] * rows[i, :PAIR, 2 * HD :].astype(F32), axis=0, keepdims=True)
        small[:RANK, :] = SCALE * total
        small[RANK:, :] = jnp.broadcast_to(mags / norms[...], (SMALL - RANK, HD))


def attend(queries, grad_attn, rows, col_scale, norms, cos, sin):
    return pl.pallas_call(
        attend_kernel,
        grid=(GROUP // HEADS,),
        in_specs=[
            pl.BlockSpec((SEQ, HEADS * HD), lambda h: (0, h)),
            pl.BlockSpec((SEQ, HEADS * HD), lambda h: (0, h)),
            whole((4, PAIR + 32, 3 * HD)),
            whole((1, HD)),
            whole((1, HD)),
            whole((SEQ, HD)),
            whole((SEQ, HD)),
        ],
        out_specs=[whole((SEQ, 2 * HD)), whole((SMALL, HD))],
        out_shape=[jax.ShapeDtypeStruct((SEQ, 2 * HD), BF), jax.ShapeDtypeStruct((SMALL, HD), F32)],
        scratch_shapes=[
            pltpu.VMEM((SEQ, 2 * HD), BF),
            pltpu.VMEM((SEQ, HD), BF),
            pltpu.VMEM((SEQ, HD), F32),
            pltpu.VMEM((SEQ, HD), F32),
        ],
        compiler_params=params(60),
        cost_estimate=cost(5 * 2 * GROUP * SEQ * SEQ * HD, 6 * MIB, GROUP * SEQ * SEQ),
        name="attend",
    )(queries, grad_attn, rows, col_scale, norms, cos, sin)


def back_kernel(
    place, grads, ups, own_key, own_val, far, one, two_a, two_b, three, _, mine, theirs, rank,
    left, weights, part, far_sems, line_sems, out_sem,
):
    chunks = near_copies(0, 0, own_key, own_val, far, weights, far_sems)
    chunks += line_copies(NEAR, NEAR, own_key, own_val, one, two_a, two_b, three, weights, line_sems)
    for chunk in chunks:
        start_all(chunk)
    first = pl.multiple_of(place[1] * 128, 128)
    second = pl.multiple_of(128 - place[1] * 128, 128)
    for r in range(4):
        slot = lax.rem(place[0] + r, 4)
        left[:128, r * 256 : (r + 1) * 256] = grads[slot, pl.ds(first, 128), :]
        left[128:, r * 256 : (r + 1) * 256] = grads[slot, pl.ds(second, 128), :]
        term = lax.dot_general(grads[slot, :, HD:], ups[r], NT, preferred_element_type=F32)
        total = term if r == 0 else total + term
    rank[...] = total
    leaving = []
    base = 0
    for i, chunk in enumerate(chunks):
        size = CHUNK if i < NEAR // CHUNK else LINE // 2
        wait_all(chunk)
        here = slice(base, base + size)
        part[:, here] = lax.dot_general(left[...], weights[here, :], NT, preferred_element_type=F32).astype(BF)
        cols = pl.ds(base, size)
        leaving += start_all(
            [
                pltpu.make_async_copy(part.at[pl.ds(128, 128), cols], theirs.at[:, cols], out_sem.at[0, i]),
                pltpu.make_async_copy(part.at[pl.ds(0, 128), cols], mine.at[:, cols], out_sem.at[1, i]),
            ]
        )
        base += size
    wait_all(leaving)


def back(place, grads, ups, w_key, w_val, far, line, after):
    count = NEAR // CHUNK
    return pl.pallas_call(
        back_kernel,
        in_specs=[smem(), in_vmem(), in_vmem()] + [any_ref()] * 8,
        out_specs=[any_ref(), any_ref(), in_vmem()],
        out_shape=[jax.ShapeDtypeStruct((128, D), BF)] * 2 + [jax.ShapeDtypeStruct((PAIR, RANK), F32)],
        scratch_shapes=[
            pltpu.VMEM((PAIR, 1024), BF),
            pltpu.VMEM((D, 1024), BF),
            pltpu.VMEM((PAIR, D), BF),
            pltpu.SemaphoreType.DMA((3, count)),
            pltpu.SemaphoreType.DMA((5, 2)),
            pltpu.SemaphoreType.DMA((2, count + 2)),
        ],
        compiler_params=params(60),
        cost_estimate=cost(0, 0),
        name="back",
    )(place, grads, ups, w_key, w_val, far, *line, after)


def join_kernel(place, rank, factor, mine, theirs, _, out, mark, one, result, sems, out_sem):
    mark[...] = jnp.zeros_like(mark)
    size = D // 8
    chunks = []
    for i in range(8):
        cols = pl.ds(i * size, size)
        chunks.append(start_all([pltpu.make_async_copy(mine.at[:, cols], one.at[:, cols], sems.at[i])]))
    own = rank[pl.ds(pl.multiple_of(place[1] * 128, 128), 128), :]
    leaving = []
    for i, chunk in enumerate(chunks):
        here = slice(i * size, (i + 1) * size)
        adapter = SCALE * jnp.dot(own, factor[:, here], preferred_element_type=F32)
        wait_all(chunk)
        result[:, here] = (one[:, here].astype(F32) + theirs[:, here].astype(F32) + adapter).astype(BF)
        cols = pl.ds(i * size, size)
        leaving += start_all([pltpu.make_async_copy(result.at[:, cols], out.at[:, cols], out_sem.at[i])])
    wait_all(leaving)


def join(place, rank, factor, mine, theirs, after):
    return pl.pallas_call(
        join_kernel,
        in_specs=[smem(), in_vmem(), whole((RANK, D)), any_ref(), in_vmem(), any_ref()],
        out_specs=[any_ref(), in_vmem()],
        out_shape=[jax.ShapeDtypeStruct((128, D), BF), jax.ShapeDtypeStruct((8, HD), F32)],
        scratch_shapes=[pltpu.VMEM((128, D), BF)] * 2 + [pltpu.SemaphoreType.DMA((8,))] * 2,
        compiler_params=params(16),
        cost_estimate=cost(0, 0),
        name="join",
    )(place, rank, factor, mine, theirs, after)


def down_kernel(place, part, got, pair, out, rank, hid, sems):
    chunks = [start_all([copy]) for copy in pair_copies(pair, hid, 0, 4, sems)]
    rank[...] = (part[...] + got[...]).astype(BF)
    lane = lax.broadcasted_iota(jnp.int32, (8, HD), 1) // 32
    core = place[1]
    size = D // 4
    for step, chunk in enumerate(chunks):
        wait_all(chunk)
        here = hid[:, step * size : (step + 1) * size]
        product = SCALE * lax.dot_general(rank[...], here, TN, preferred_element_type=F32)
        for tile in range(size // HD):
            regs = [product[8 * i : 8 * i + 8, tile * HD : (tile + 1) * HD] for i in range(4)]
            blocks = []
            for pick in range(2):
                column = 2 * pick + core
                block = jnp.zeros((8, HD), F32)
                for i in range(4):
                    moved = pltpu.roll(regs[i], lax.rem((i - column + 4) * 32, HD), 1)
                    block = jnp.where(lane == i, moved, block)
                blocks.append(block)
            first = step * (size // 8) + 16 * tile
            out[first : first + 16, :] = jnp.concatenate(blocks, axis=0).astype(BF)


def down_part(place, part, got, pair):
    return pl.pallas_call(
        down_kernel,
        in_specs=[smem(), in_vmem(), in_vmem(), any_ref()],
        out_specs=[whole((1024, HD)), in_vmem()],
        out_shape=[jax.ShapeDtypeStruct((1024, HD), BF), jax.ShapeDtypeStruct((PAIR, RANK), BF)],
        scratch_shapes=[pltpu.VMEM((PAIR, D), BF), pltpu.SemaphoreType.DMA((4,))],
        compiler_params=params(58),
        cost_estimate=cost(2 * PAIR * D * RANK, 5 * MIB),
        name="down_part",
    )(place, part, got, pair)


def fold_kernel(small, out):
    out[...] = jnp.sum(small[...], axis=0)


def fold(small):
    return pl.pallas_call(
        fold_kernel,
        grid=(1,),
        in_specs=[whole((16, 40, HD))],
        out_specs=whole((40, HD)),
        out_shape=jax.ShapeDtypeStruct((40, HD), F32),
        compiler_params=params(60),
        cost_estimate=cost(0, 0),
        name="fold",
    )(small)


def finish_kernel(pieces, small, other, _, out, up_grad, mag_grad):
    total = jnp.sum(pieces[...].astype(F32).reshape(128, 8, HD), axis=0)
    for i in range(4):
        out[8 * i : 8 * i + 8, :] = total[:, 32 * i : 32 * i + 32]
    sums = small[...] + other[...]
    up_grad[...] = sums[:RANK]
    mag_grad[...] = sums[RANK : RANK + 1]


def finish(pieces, small, other, after):
    return pl.pallas_call(
        finish_kernel,
        in_specs=[in_vmem(), in_vmem(), in_vmem(), any_ref()],
        out_specs=[whole((RANK, 32)), whole((RANK, HD)), whole((1, HD))],
        out_shape=[
            jax.ShapeDtypeStruct((RANK, 32), F32),
            jax.ShapeDtypeStruct((RANK, HD), F32),
            jax.ShapeDtypeStruct((1, HD), F32),
        ],
        compiler_params=params(8),
        cost_estimate=cost(0, 0),
        name="finish",
    )(pieces, small, other, after)


def along_z(value, shift):
    return lax.ppermute(value, ("zh", "zl"), [(i, (i + shift) % 8) for i in range(8)])


def gather_weights(w_key, w_val, up):
    count = NEAR // 16
    at = (lax.axis_index("x") * 4 + lax.axis_index("y")) * count
    seed = jnp.concatenate([lax.dynamic_slice(w, (at, 0), (count, HD)) for w in (w_key, w_val)], axis=1)
    half = count // 2
    first = along_z(seed, -1)
    third = along_z(seed, 1)
    second = jnp.concatenate([along_z(seed[:half], -2), along_z(seed[half:], 2)], axis=0)
    far = lax.all_gather(jnp.concatenate([first, second, third], axis=1), ("x", "y"), axis=0, tiled=True)
    own = jnp.concatenate([w_key[NEAR:], w_val[NEAR:]], axis=1)
    own = jnp.concatenate([jnp.pad(up, ((0, 0), (0, HD))), own], axis=0) + seed[:1, :1] * 0
    one = along_z(own, -1)
    three = along_z(own, 1)
    two_a = along_z(one[: RANK + LINE // 2], -1)
    two_b = along_z(three[RANK + LINE // 2 :], 1)
    ups = jnp.stack([up] + [got[:RANK, :HD] for got in (one, two_a, three)])
    return far, (one, two_a, two_b, three), ups


def shards(hidden, w_key, w_val, factor, up, mag, queries, grad_attn):
    zl, core = lax.axis_index("zl"), lax.axis_index("core")
    place = jnp.stack([zl, core]).astype(jnp.int32)
    swap = [(0, 1), (1, 0)]
    other = lax.ppermute(hidden, "core", swap)
    pair = jnp.where(
        core == 0, jnp.concatenate([hidden, other], axis=0), jnp.concatenate([other, hidden], axis=0)
    )
    down = lax.dot_general(pair, factor, NT, preferred_element_type=F32).astype(BF)
    far, line, ups = gather_weights(w_key, w_val, up)
    merged = w_val.astype(F32) + SCALE * lax.dot_general(factor, up, TN, preferred_element_type=F32)
    norms = jnp.sqrt(jnp.sum(merged * merged, axis=0))
    col_scale = (mag / norms).reshape(1, HD)
    cos, sin = rope_tables()
    cos_here = lax.dynamic_slice(cos, (zl * PAIR, 0), (PAIR, HD))
    sin_here = lax.dynamic_slice(sin, (zl * PAIR, 0), (PAIR, HD))
    so_far = project_line(pair, w_key, w_val, line)
    rows = project(place, pair, w_key, w_val, far, so_far, down, ups, cos_here, sin_here)
    rows = lax.all_to_all(rows, "zl", 0, 0, tiled=True)
    grads, small = attend(queries, grad_attn, rows, col_scale, norms.reshape(1, HD), cos, sin)
    grads = lax.all_to_all(grads.reshape(4, PAIR, 2 * HD), "zl", 0, 0, tiled=True)
    gathered = lax.all_gather(small, ("x", "y"), axis=0, tiled=True)
    mine, theirs, part = back(place, grads, ups, w_key, w_val, far, line, small)
    got = lax.ppermute(part, "core", swap)
    theirs = lax.ppermute(theirs, "core", swap)
    pieces, rank = down_part(place, part, got, pair)
    pieces = lax.all_to_all(pieces, DP + ("zl",), 0, 0, tiled=True)
    small = fold(gathered.reshape(16, SMALL, HD))
    other = lax.ppermute(small, "zh", swap)
    grad_hidden, mark = join(place, rank, factor, mine, theirs, small)
    grad_down, up_sum, mag_sum = finish(pieces, small, other, mark)
    return grad_hidden, grad_down, up_sum, mag_sum.reshape(HD)


def solution(mesh):
    fine = Mesh(np.asarray(mesh.devices).reshape(4, 4, 2, 4, 2), EVERY)
    tensor = ("zl", "core")
    return jax.shard_map(
        shards,
        mesh=fine,
        in_specs=(
            P(EVERY, None),
            P(None, tensor),
            P(None, tensor),
            P(),
            P(None, tensor),
            P(tensor),
            P(DP, tensor),
            P(DP, tensor),
        ),
        out_specs=(P(EVERY, None), P(None, EVERY), P(None, tensor), P(tensor)),
        check_vma=False,
    )
```

```python
import jax
import jax.numpy as jnp
import numpy as np
from jax import lax
from jax.experimental import pallas as pl
from jax.experimental.pallas import tpu as pltpu
from jax.sharding import Mesh, PartitionSpec as P

HD = 128
D = 8192
SEQ = 1024
RANK = 32
PAIR = 256
NEAR = 5120
LINE = 3072
CHUNK = 1280
QB = 256
GROUP = 4
HEADS = 2
SMALL = 256
SCALE = 2.0
ROPE_BASE = 500000.0
LOG2E = 1.4426950408889634
INV_SQRT = HD ** (-0.5)
MIB = 1024 * 1024
BF = jnp.bfloat16
F32 = jnp.float32
NT = (((1,), (1,)), ((), ()))
TN = (((0,), (0,)), ((), ()))
EVERY = ("x", "y", "zh", "zl", "core")
DP = ("x", "y", "zh")


def rope_tables():
    half = HD // 2
    frequency = ROPE_BASE ** (-(jnp.arange(half, dtype=F32) * 2.0 / HD))
    angles = jnp.arange(SEQ, dtype=F32)[:, None] * frequency[None, :]
    cosine, sine = jnp.cos(angles), jnp.sin(angles)
    return jnp.concatenate([cosine, cosine], 1), jnp.concatenate([-sine, sine], 1)


def smem():
    return pl.BlockSpec(memory_space=pltpu.SMEM)


def whole(shape):
    return pl.BlockSpec(shape, lambda *_: (0,) * len(shape))


def params(limit):
    return pltpu.CompilerParams(vmem_limit_bytes=limit * MIB)


def cost(flops, moved, trans=0):
    return pl.CostEstimate(flops=flops, bytes_accessed=moved, transcendentals=trans)


def in_vmem():
    return pl.BlockSpec(memory_space=pltpu.VMEM)


def any_ref():
    return pl.BlockSpec(memory_space=pl.ANY)


def start_all(copies):
    for copy in copies:
        copy.start()
    return copies


def wait_all(copies):
    for copy in copies:
        copy.wait()


def near_copies(base, first, own_key, own_val, far, weights, sems):
    chunks = []
    for i in range(far.shape[0] // CHUNK):
        here = pl.ds(first + i * CHUNK, CHUNK)
        near = pl.ds(i * CHUNK, CHUNK)
        there = pl.ds(base + i * CHUNK, CHUNK)
        chunks.append(
            [
                pltpu.make_async_copy(own_key.at[there, :], weights.at[here, pl.ds(0, HD)], sems.at[0, i]),
                pltpu.make_async_copy(own_val.at[there, :], weights.at[here, pl.ds(HD, HD)], sems.at[1, i]),
                pltpu.make_async_copy(far.at[near, :], weights.at[here, pl.ds(256, 768)], sems.at[2, i]),
            ]
        )
    return chunks


def line_copies(base, first, own_key, own_val, one, two_a, two_b, three, weights, sems):
    chunks = []
    size = LINE // 2
    for i, two in enumerate((two_a.at[pl.ds(RANK, size), :], two_b)):
        here = pl.ds(first + i * size, size)
        there = pl.ds(base + i * size, size)
        near = pl.ds(RANK + i * size, size)
        chunks.append(
            [
                pltpu.make_async_copy(own_key.at[there, :], weights.at[here, pl.ds(0, HD)], sems.at[0, i]),
                pltpu.make_async_copy(own_val.at[there, :], weights.at[here, pl.ds(HD, HD)], sems.at[1, i]),
                pltpu.make_async_copy(one.at[near, :], weights.at[here, pl.ds(256, 256)], sems.at[2, i]),
                pltpu.make_async_copy(two, weights.at[here, pl.ds(512, 256)], sems.at[3, i]),
                pltpu.make_async_copy(three.at[near, :], weights.at[here, pl.ds(768, 256)], sems.at[4, i]),
            ]
        )
    return chunks


def pair_copies(pair, hid, base, count, sem):
    size = hid.shape[1] // count
    return [
        pltpu.make_async_copy(
            pair.at[:, pl.ds(base + i * size, size)], hid.at[:, pl.ds(i * size, size)], sem.at[i]
        )
        for i in range(count)
    ]


def multiply(acc, chunks, hid_chunks, hid, weights):
    size = hid.shape[1] // len(chunks)
    for i, chunk in enumerate(chunks):
        wait_all(chunk + [hid_chunks[i]])
        here = slice(i * size, (i + 1) * size)
        term = jnp.dot(hid[:, here], weights[here, :], preferred_element_type=F32)
        acc = term if acc is None else acc + term
    return acc


def project_line_kernel(
    pair, own_key, own_val, one, two_a, two_b, three, out, hid, weights, hid_sem, sems
):
    chunks = line_copies(NEAR, 0, own_key, own_val, one, two_a, two_b, three, weights, sems)
    hid_chunks = pair_copies(pair, hid, NEAR, 2, hid_sem)
    for i in range(2):
        start_all(chunks[i] + [hid_chunks[i]])
    out[...] = multiply(None, chunks, hid_chunks, hid, weights)


def project_line(pair, w_key, w_val, line):
    return pl.pallas_call(
        project_line_kernel,
        in_specs=[any_ref()] * 7,
        out_specs=whole((PAIR, 1024)),
        out_shape=jax.ShapeDtypeStruct((PAIR, 1024), F32),
        scratch_shapes=[
            pltpu.VMEM((PAIR, LINE), BF),
            pltpu.VMEM((LINE, 1024), BF),
            pltpu.SemaphoreType.DMA((2,)),
            pltpu.SemaphoreType.DMA((5, 2)),
        ],
        compiler_params=params(60),
        cost_estimate=cost(2 * PAIR * LINE * 1024, 8 * MIB),
        name="project_line",
    )(pair, w_key, w_val, *line)


def project_kernel(
    place, pair, own_key, own_val, far, so_far, down, ups, cos, sin, out, hid, weights, hid_sem, sems
):
    count = NEAR // CHUNK
    chunks = near_copies(0, 0, own_key, own_val, far, weights, sems)
    hid_chunks = pair_copies(pair, hid, 0, count, hid_sem)
    for i in range(count):
        start_all(chunks[i] + [hid_chunks[i]])
    acc = multiply(so_far[...], chunks, hid_chunks, hid, weights)
    packed = jnp.concatenate([down[64 * j : 64 * j + 64, :] for j in range(4)], axis=1)
    packed = jnp.concatenate([packed[:32], packed[32:], jnp.zeros((32, HD), BF)], axis=1)
    for r in range(4):
        key = acc[:, r * 256 : r * 256 + HD]
        turned = key * cos[...] + pltpu.roll(key, HD // 2, 1) * sin[...]
        turned = turned * (INV_SQRT * LOG2E)
        high = turned.astype(BF)
        low = (turned - high.astype(F32)).astype(BF)
        lifted = jnp.dot(down[...], ups[r], preferred_element_type=F32)
        base = (acc[:, r * 256 + HD : (r + 1) * 256] + SCALE * lifted).astype(BF)
        slot = lax.rem(place[0] + r, 4)
        out[slot, :PAIR, :] = jnp.concatenate([high, low, base], axis=1)
        out[slot, PAIR:, :] = packed


def project(place, pair, w_key, w_val, far, so_far, down, ups, cos, sin):
    count = NEAR // CHUNK
    return pl.pallas_call(
        project_kernel,
        in_specs=[
            smem(),
            any_ref(),
            any_ref(),
            any_ref(),
            any_ref(),
            whole((PAIR, 1024)),
            whole((PAIR, RANK)),
            whole((4, RANK, HD)),
            whole((PAIR, HD)),
            whole((PAIR, HD)),
        ],
        out_specs=whole((4, PAIR + 32, 3 * HD)),
        out_shape=jax.ShapeDtypeStruct((4, PAIR + 32, 3 * HD), BF),
        scratch_shapes=[
            pltpu.VMEM((PAIR, NEAR), BF),
            pltpu.VMEM((NEAR, 1024), BF),
            pltpu.SemaphoreType.DMA((count,)),
            pltpu.SemaphoreType.DMA((3, count)),
        ],
        compiler_params=params(60),
        cost_estimate=cost(2 * PAIR * NEAR * 1024, 14 * MIB),
        name="project",
    )(place, pair, w_key, w_val, far, so_far, down, ups, cos, sin)


def attend_kernel(query, grad, rows, col_scale, norms, cos_far, sin_far, grads, small, keys, vals, dkey, dval, cos, sin, sems):
    step = pl.program_id(0)
    tables = [pltpu.make_async_copy(cos_far, cos, sems.at[0]), pltpu.make_async_copy(sin_far, sin, sems.at[1])]

    @pl.when(step == 0)
    def _():
        for i in range(4):
            here = slice(i * PAIR, (i + 1) * PAIR)
            keys[here, :] = rows[i, :PAIR, : 2 * HD]
            vals[here, :] = (rows[i, :PAIR, 2 * HD :].astype(F32) * col_scale[...]).astype(BF)
        dkey[...] = jnp.zeros_like(dkey)
        dval[...] = jnp.zeros_like(dval)
        start_all(tables)

    for block in range(SEQ // QB):
        stop = (block + 1) * QB
        here = slice(block * QB, stop)
        queries, outs, halves, sgrads = [], [], [], []
        for head in range(HEADS):
            q = query[here, head * HD : (head + 1) * HD]
            g = grad[here, head * HD : (head + 1) * HD]
            qq = jnp.concatenate([q, q], axis=1)
            scores = lax.dot_general(keys[:stop], qq, NT, preferred_element_type=F32)
            key_at = lax.broadcasted_iota(jnp.int32, (QB, QB), 0)
            query_at = lax.broadcasted_iota(jnp.int32, (QB, QB), 1)
            edge = jnp.where(key_at <= query_at, scores[block * QB :], -1e30)
            if block:
                scores = jnp.concatenate([scores[: block * QB], edge], axis=0)
            else:
                scores = edge
            powers = jnp.exp2(scores - jnp.max(scores, axis=0, keepdims=True))
            attn = powers * (1.0 / jnp.sum(powers, axis=0, keepdims=True))
            half = attn.astype(BF)
            pgrad = lax.dot_general(vals[:stop], g, NT, preferred_element_type=F32)
            delta = jnp.sum(half.astype(F32) * pgrad, axis=0, keepdims=True)
            sgrads.append((attn * (pgrad - delta)).astype(BF))
            halves.append(half)
            queries.append(q)
            outs.append(g)
        dval[:stop] += jnp.dot(
            jnp.concatenate(halves, 1), jnp.concatenate(outs, 0), preferred_element_type=F32
        )
        dkey[:stop] += jnp.dot(
            jnp.concatenate(sgrads, 1), jnp.concatenate(queries, 0), preferred_element_type=F32
        )

    @pl.when(step == pl.num_programs(0) - 1)
    def _():
        wait_all(tables)
        dk = dkey[...] * INV_SQRT
        dk = dk * cos[...] - pltpu.roll(dk, HD // 2, 1) * sin[...]
        dv = dval[...]
        gv = (dv * col_scale[...]).astype(BF)
        grads[:, :HD] = dk.astype(BF)
        grads[:, HD:] = gv
        total = jnp.zeros((RANK, HD), F32)
        mags = jnp.zeros((1, HD), F32)
        for i in range(4):
            here = slice(i * PAIR, (i + 1) * PAIR)
            packed = rows[i, PAIR:, : 2 * HD]
            packed = jnp.concatenate([packed[:, :HD], packed[:, HD:]], axis=0)
            down = jnp.concatenate([packed[:, 32 * j : 32 * j + 32] for j in range(4)], axis=0)
            total += lax.dot_general(down, gv[here], TN, preferred_element_type=F32)
            mags += jnp.sum(dv[here] * rows[i, :PAIR, 2 * HD :].astype(F32), axis=0, keepdims=True)
        small[:RANK, :] = SCALE * total
        small[RANK:, :] = jnp.broadcast_to(mags / norms[...], (SMALL - RANK, HD))


def attend(queries, grad_attn, rows, col_scale, norms, cos, sin):
    return pl.pallas_call(
        attend_kernel,
        grid=(GROUP // HEADS,),
        in_specs=[
            pl.BlockSpec((SEQ, HEADS * HD), lambda h: (0, h)),
            pl.BlockSpec((SEQ, HEADS * HD), lambda h: (0, h)),
            whole((4, PAIR + 32, 3 * HD)),
            whole((1, HD)),
            whole((1, HD)),
            any_ref(),
            any_ref(),
        ],
        out_specs=[whole((SEQ, 2 * HD)), whole((SMALL, HD))],
        out_shape=[jax.ShapeDtypeStruct((SEQ, 2 * HD), BF), jax.ShapeDtypeStruct((SMALL, HD), F32)],
        scratch_shapes=[
            pltpu.VMEM((SEQ, 2 * HD), BF),
            pltpu.VMEM((SEQ, HD), BF),
            pltpu.VMEM((SEQ, HD), F32),
            pltpu.VMEM((SEQ, HD), F32),
            pltpu.VMEM((SEQ, HD), F32),
            pltpu.VMEM((SEQ, HD), F32),
            pltpu.SemaphoreType.DMA((2,)),
        ],
        compiler_params=params(60),
        cost_estimate=cost(5 * 2 * GROUP * SEQ * SEQ * HD, 6 * MIB, GROUP * SEQ * SEQ),
        name="attend",
    )(queries, grad_attn, rows, col_scale, norms, cos, sin)


def back_kernel(
    place, grads, ups, own_key, own_val, far, one, two_a, two_b, three, _, mine, theirs, rank,
    left, weights, part, far_sems, line_sems, out_sem,
):
    chunks = near_copies(0, 0, own_key, own_val, far, weights, far_sems)
    chunks += line_copies(NEAR, NEAR, own_key, own_val, one, two_a, two_b, three, weights, line_sems)
    for chunk in chunks:
        start_all(chunk)
    first = pl.multiple_of(place[1] * 128, 128)
    second = pl.multiple_of(128 - place[1] * 128, 128)
    for r in range(4):
        slot = lax.rem(place[0] + r, 4)
        left[:128, r * 256 : (r + 1) * 256] = grads[slot, pl.ds(first, 128), :]
        left[128:, r * 256 : (r + 1) * 256] = grads[slot, pl.ds(second, 128), :]
        term = lax.dot_general(grads[slot, :, HD:], ups[r], NT, preferred_element_type=F32)
        total = term if r == 0 else total + term
    rank[...] = total
    leaving = []
    base = 0
    for i, chunk in enumerate(chunks):
        size = CHUNK if i < NEAR // CHUNK else LINE // 2
        wait_all(chunk)
        here = slice(base, base + size)
        part[:, here] = lax.dot_general(left[...], weights[here, :], NT, preferred_element_type=F32).astype(BF)
        cols = pl.ds(base, size)
        leaving += start_all(
            [
                pltpu.make_async_copy(part.at[pl.ds(128, 128), cols], theirs.at[:, cols], out_sem.at[0, i]),
                pltpu.make_async_copy(part.at[pl.ds(0, 128), cols], mine.at[:, cols], out_sem.at[1, i]),
            ]
        )
        base += size
    wait_all(leaving)


def back(place, grads, ups, w_key, w_val, far, line, after):
    count = NEAR // CHUNK
    return pl.pallas_call(
        back_kernel,
        in_specs=[smem(), in_vmem(), in_vmem()] + [any_ref()] * 8,
        out_specs=[any_ref(), any_ref(), in_vmem()],
        out_shape=[jax.ShapeDtypeStruct((128, D), BF)] * 2 + [jax.ShapeDtypeStruct((PAIR, RANK), F32)],
        scratch_shapes=[
            pltpu.VMEM((PAIR, 1024), BF),
            pltpu.VMEM((D, 1024), BF),
            pltpu.VMEM((PAIR, D), BF),
            pltpu.SemaphoreType.DMA((3, count)),
            pltpu.SemaphoreType.DMA((5, 2)),
            pltpu.SemaphoreType.DMA((2, count + 2)),
        ],
        compiler_params=params(60),
        cost_estimate=cost(0, 0),
        name="back",
    )(place, grads, ups, w_key, w_val, far, *line, after)


def join_kernel(place, rank, factor, mine, theirs, _, out, mark, one, result, sems, out_sem):
    mark[...] = jnp.zeros_like(mark)
    size = D // 8
    chunks = []
    for i in range(8):
        cols = pl.ds(i * size, size)
        chunks.append(start_all([pltpu.make_async_copy(mine.at[:, cols], one.at[:, cols], sems.at[i])]))
    own = rank[pl.ds(pl.multiple_of(place[1] * 128, 128), 128), :]
    leaving = []
    for i, chunk in enumerate(chunks):
        here = slice(i * size, (i + 1) * size)
        adapter = SCALE * jnp.dot(own, factor[:, here], preferred_element_type=F32)
        wait_all(chunk)
        result[:, here] = (one[:, here].astype(F32) + theirs[:, here].astype(F32) + adapter).astype(BF)
        cols = pl.ds(i * size, size)
        leaving += start_all([pltpu.make_async_copy(result.at[:, cols], out.at[:, cols], out_sem.at[i])])
    wait_all(leaving)


def join(place, rank, factor, mine, theirs, after):
    return pl.pallas_call(
        join_kernel,
        in_specs=[smem(), in_vmem(), whole((RANK, D)), any_ref(), in_vmem(), any_ref()],
        out_specs=[any_ref(), in_vmem()],
        out_shape=[jax.ShapeDtypeStruct((128, D), BF), jax.ShapeDtypeStruct((8, HD), F32)],
        scratch_shapes=[pltpu.VMEM((128, D), BF)] * 2 + [pltpu.SemaphoreType.DMA((8,))] * 2,
        compiler_params=params(16),
        cost_estimate=cost(0, 0),
        name="join",
    )(place, rank, factor, mine, theirs, after)


def down_kernel(place, part, got, pair, out, rank, hid, sems):
    chunks = [start_all([copy]) for copy in pair_copies(pair, hid, 0, 4, sems)]
    rank[...] = (part[...] + got[...]).astype(BF)
    lane = lax.broadcasted_iota(jnp.int32, (8, HD), 1) // 32
    core = place[1]
    size = D // 4
    for step, chunk in enumerate(chunks):
        wait_all(chunk)
        here = hid[:, step * size : (step + 1) * size]
        product = SCALE * lax.dot_general(rank[...], here, TN, preferred_element_type=F32)
        for tile in range(size // HD):
            regs = [product[8 * i : 8 * i + 8, tile * HD : (tile + 1) * HD] for i in range(4)]
            blocks = []
            for pick in range(2):
                column = 2 * pick + core
                block = jnp.zeros((8, HD), F32)
                for i in range(4):
                    moved = pltpu.roll(regs[i], lax.rem((i - column + 4) * 32, HD), 1)
                    block = jnp.where(lane == i, moved, block)
                blocks.append(block)
            first = step * (size // 8) + 16 * tile
            out[first : first + 16, :] = jnp.concatenate(blocks, axis=0).astype(BF)


def down_part(place, part, got, pair):
    return pl.pallas_call(
        down_kernel,
        in_specs=[smem(), in_vmem(), in_vmem(), any_ref()],
        out_specs=[whole((1024, HD)), in_vmem()],
        out_shape=[jax.ShapeDtypeStruct((1024, HD), BF), jax.ShapeDtypeStruct((PAIR, RANK), BF)],
        scratch_shapes=[pltpu.VMEM((PAIR, D), BF), pltpu.SemaphoreType.DMA((4,))],
        compiler_params=params(58),
        cost_estimate=cost(2 * PAIR * D * RANK, 5 * MIB),
        name="down_part",
    )(place, part, got, pair)


def fold_kernel(small, out):
    out[...] = jnp.sum(small[...], axis=0)


def fold(small):
    return pl.pallas_call(
        fold_kernel,
        grid=(1,),
        in_specs=[whole((16, 40, HD))],
        out_specs=whole((40, HD)),
        out_shape=jax.ShapeDtypeStruct((40, HD), F32),
        compiler_params=params(60),
        cost_estimate=cost(0, 0),
        name="fold",
    )(small)


def finish_kernel(pieces, small, other, _, out, up_grad, mag_grad):
    total = jnp.sum(pieces[...].astype(F32).reshape(128, 8, HD), axis=0)
    for i in range(4):
        out[8 * i : 8 * i + 8, :] = total[:, 32 * i : 32 * i + 32]
    sums = small[...] + other[...]
    up_grad[...] = sums[:RANK]
    mag_grad[...] = sums[RANK : RANK + 1]


def finish(pieces, small, other, after):
    return pl.pallas_call(
        finish_kernel,
        in_specs=[in_vmem(), in_vmem(), in_vmem(), any_ref()],
        out_specs=[whole((RANK, 32)), whole((RANK, HD)), whole((1, HD))],
        out_shape=[
            jax.ShapeDtypeStruct((RANK, 32), F32),
            jax.ShapeDtypeStruct((RANK, HD), F32),
            jax.ShapeDtypeStruct((1, HD), F32),
        ],
        compiler_params=params(8),
        cost_estimate=cost(0, 0),
        name="finish",
    )(pieces, small, other, after)


def along_z(value, shift):
    return lax.ppermute(value, ("zh", "zl"), [(i, (i + shift) % 8) for i in range(8)])


def gather_weights(w_key, w_val, up):
    count = NEAR // 16
    at = (lax.axis_index("x") * 4 + lax.axis_index("y")) * count
    seed = jnp.concatenate([lax.dynamic_slice(w, (at, 0), (count, HD)) for w in (w_key, w_val)], axis=1)
    half = count // 2
    first = along_z(seed, -1)
    third = along_z(seed, 1)
    second = jnp.concatenate([along_z(seed[:half], -2), along_z(seed[half:], 2)], axis=0)
    far = lax.all_gather(jnp.concatenate([first, second, third], axis=1), ("x", "y"), axis=0, tiled=True)
    own = jnp.concatenate([w_key[NEAR:], w_val[NEAR:]], axis=1)
    own = jnp.concatenate([jnp.pad(up, ((0, 0), (0, HD))), own], axis=0) + seed[:1, :1] * 0
    one = along_z(own, -1)
    three = along_z(own, 1)
    two_a = along_z(one[: RANK + LINE // 2], -1)
    two_b = along_z(three[RANK + LINE // 2 :], 1)
    ups = jnp.stack([up] + [got[:RANK, :HD] for got in (one, two_a, three)])
    return far, (one, two_a, two_b, three), ups


def shards(hidden, w_key, w_val, factor, up, mag, queries, grad_attn):
    zl, core = lax.axis_index("zl"), lax.axis_index("core")
    place = jnp.stack([zl, core]).astype(jnp.int32)
    swap = [(0, 1), (1, 0)]
    other = lax.ppermute(hidden, "core", swap)
    pair = jnp.where(
        core == 0, jnp.concatenate([hidden, other], axis=0), jnp.concatenate([other, hidden], axis=0)
    )
    down = lax.dot_general(pair, factor, NT, preferred_element_type=F32).astype(BF)
    far, line, ups = gather_weights(w_key, w_val, up)
    merged = w_val.astype(F32) + SCALE * lax.dot_general(factor, up, TN, preferred_element_type=F32)
    norms = jnp.sqrt(jnp.sum(merged * merged, axis=0))
    col_scale = (mag / norms).reshape(1, HD)
    cos, sin = rope_tables()
    cos_here = lax.dynamic_slice(cos, (zl * PAIR, 0), (PAIR, HD))
    sin_here = lax.dynamic_slice(sin, (zl * PAIR, 0), (PAIR, HD))
    so_far = project_line(pair, w_key, w_val, line)
    rows = project(place, pair, w_key, w_val, far, so_far, down, ups, cos_here, sin_here)
    rows = lax.all_to_all(rows, "zl", 0, 0, tiled=True)
    grads, small = attend(queries, grad_attn, rows, col_scale, norms.reshape(1, HD), cos, sin)
    grads = lax.all_to_all(grads.reshape(4, PAIR, 2 * HD), "zl", 0, 0, tiled=True)
    gathered = lax.all_gather(small, ("x", "y"), axis=0, tiled=True)
    mine, theirs, part = back(place, grads, ups, w_key, w_val, far, line, small)
    got = lax.ppermute(part, "core", swap)
    theirs = lax.ppermute(theirs, "core", swap)
    pieces, rank = down_part(place, part, got, pair)
    pieces = lax.all_to_all(pieces, DP + ("zl",), 0, 0, tiled=True)
    small = fold(gathered.reshape(16, SMALL, HD))
    other = lax.ppermute(small, "zh", swap)
    grad_hidden, mark = join(place, rank, factor, mine, theirs, small)
    grad_down, up_sum, mag_sum = finish(pieces, small, other, mark)
    return grad_hidden, grad_down, up_sum, mag_sum.reshape(HD)


def solution(mesh):
    fine = Mesh(np.asarray(mesh.devices).reshape(4, 4, 2, 4, 2), EVERY)
    tensor = ("zl", "core")
    return jax.shard_map(
        shards,
        mesh=fine,
        in_specs=(
            P(EVERY, None),
            P(None, tensor),
            P(None, tensor),
            P(),
            P(None, tensor),
            P(tensor),
            P(DP, tensor),
            P(DP, tensor),
        ),
        out_specs=(P(EVERY, None), P(None, EVERY), P(None, tensor), P(tensor)),
        check_vma=False,
    )
```
